32 devices in a mesh: tm: 8 (over y, x, core), space: 4 (over z).
Axes of the slice: x: 2, y: 2, z: 4, core: 2. Of those that a mesh axis runs over, the one named last changes fastest.
Arguments:
- query: bfloat16 [8, 512, 1536], P('tm', 'space')
- key_new: bfloat16 [8, 512, 1536], P('tm', 'space')
- value_new: bfloat16 [8, 512, 1536], P('tm', 'space'), may hold values from -6 to 6
- key_clean: bfloat16 [8, 512, 1536], P('tm', 'space'), may hold values from -6 to 6
- value_clean: bfloat16 [8, 512, 1536], P('tm', 'space'), may hold values from -6 to 6
- out_weight: bfloat16 [1536, 1536], replicated, may hold values from -1.25 to 1.25
- step_gate: float32 [4, 1536], replicated, may hold values from 0.5 to 1.5
- noise_step: int32 [8], P('tm'), may hold values from 0 to 3
- tile_mask: int32 [8, 4, 3], P('tm', 'space'), may hold values 0 or 1
Outputs:
- gated_out: bfloat16 [8, 512, 1536], P('tm', 'space')
The draws below stay inside these ranges and needn't reach their ends.
All inputs are finite; a program needn't handle non-finite values. No bound on the sum of `tile_mask` on one device may be relied on, other than what follows from the above.
Results may differ from the reference program's by a relative error of at most 0.0075.
Values may be sent and summed in bfloat16 or wider, within the bound.
A program may use at most 64 MiB of HBM per device.

```python
import math
import jax
import jax.numpy as jnp
from jax import lax

D = 1536
HEADS = 12
HEAD = 128
TILE = 128
PAST = 3
STEPS = 4
GROUPS = 8
TOKC = 512
TILES = 4


def paired_keys(key):
    return jnp.clip(jax.random.normal(jax.random.fold_in(key, 11), (GROUPS, TOKC, D), jnp.float32), -6.0, 6.0)


def draw_key_new(key, part):
    base = paired_keys(key)
    return base.astype(jnp.bfloat16)


def draw_query(key, part):
    drawn = jnp.clip(1.5 * jax.random.normal(jax.random.fold_in(key, 12), (GROUPS, TOKC, D), jnp.float32), -9.0, 9.0)
    return drawn.astype(jnp.bfloat16)


def with_ends(drawn, stream_key, low, largest):
    dims = drawn.shape
    index_at = [jax.random.randint(jax.random.fold_in(stream_key, axis), (), 0, dims[axis]) for axis in range(len(dims))]
    drawn = drawn.at[tuple(index_at)].set(low)
    longest = dims.index(max(dims))
    index_at[longest] = (index_at[longest] + 1) % dims[longest]
    return drawn.at[tuple(index_at)].set(largest)


def block_levels(key, extent, shards, smallest, high):
    gain = 1.0
    for dim, shards_of in shards:
        draws = jax.random.uniform(jax.random.fold_in(jax.random.fold_in(key, 6), dim), (shards_of,), jnp.float32, smallest / len(shards), high / len(shards))
        gain = gain * jnp.repeat(jnp.exp(draws), extent[dim] // shards_of).reshape((-1,) + (1,) * (len(extent) - 1 - dim))
    return gain


def centred(own_key, dims, spread, bound, split=(), held_as=jnp.bfloat16):
    values = jax.random.normal(own_key, dims, jnp.float32) * spread
    if len(split) > 0:
        values = block_levels(own_key, dims, split, -0.22, 0.18) * values
    return jnp.clip(values, min=-bound, max=bound).astype(held_as)


def setup_inputs(seed: int = 0) -> dict:
    seeds = jax.random.split(jax.random.key(seed), 10)
    return {
        "query": draw_query(jax.random.fold_in(seeds[9], 71), 0),
        "key_new": draw_key_new(jax.random.fold_in(seeds[9], 71), 0),
        "value_new": centred(seeds[2], (GROUPS, TOKC, D), 1.0, 6.0, ((0, 8), (1, 4))),
        "key_clean": centred(seeds[3], (GROUPS, TOKC, D), 1.0, 6.0, ((0, 8), (1, 4))),
        "value_clean": centred(seeds[4], (GROUPS, TOKC, D), 1.0, 6.0, ((0, 8), (1, 4))),
        "out_weight": centred(seeds[5], (D, D), (D // 64) ** -0.5, 1.25),
        "step_gate": jnp.clip(jax.random.uniform(seeds[6], (STEPS, D), jnp.float32, 0.5, 1.5), 0.5, 1.5),
        "noise_step": with_ends(jax.random.randint(seeds[7], (GROUPS,), 0, STEPS), jax.random.fold_in(seeds[7], 1), 0, STEPS - 1).astype(jnp.int32),
        "tile_mask": with_ends((jax.random.randint(seeds[8], (GROUPS, TILES, 3), 0, 3) < 2).astype(jnp.int32), jax.random.fold_in(seeds[8], 1), 0, 1),
    }


def reference(query, key_new, value_new, key_clean, value_clean, out_weight, step_gate, noise_step, tile_mask):
    group_count = query.shape[0]
    token_count = query.shape[1]
    tile_count = token_count // TILE
    score_scale = 1.0 / math.sqrt(HEAD)
    zero = jnp.zeros((), jnp.int32)
    new_keys = jnp.pad(key_new, ((0, 0), (TILE, TILE), (0, 0)))
    new_values = jnp.pad(value_new, ((0, 0), (TILE, TILE), (0, 0)))
    old_keys = jnp.pad(key_clean, ((PAST, 0), (TILE, TILE), (0, 0)))
    old_values = jnp.pad(value_clean, ((PAST, 0), (TILE, TILE), (0, 0)))

    def one_tile(flat_index):
        group = (flat_index // tile_count).astype(jnp.int32)
        tile = (flat_index % tile_count).astype(jnp.int32)
        start = (tile * TILE).astype(jnp.int32)
        query_rows = lax.dynamic_slice(query, (group, start, zero), (1, TILE, D))[0].reshape(TILE, HEADS, HEAD)
        own_keys = lax.dynamic_slice(new_keys, (group, start, zero), (1, 3 * TILE, D))[0]
        own_values = lax.dynamic_slice(new_values, (group, start, zero), (1, 3 * TILE, D))[0]
        past_keys = lax.dynamic_slice(old_keys, (group, start, zero), (PAST, 3 * TILE, D)).reshape(PAST * 3 * TILE, D)
        past_values = lax.dynamic_slice(old_values, (group, start, zero), (PAST, 3 * TILE, D)).reshape(PAST * 3 * TILE, D)
        tile_row = lax.dynamic_slice(tile_mask, (group, tile, zero), (1, 1, 3))[0, 0]
        spots = jnp.arange(3, dtype=jnp.int32)
        target = tile + spots - 1
        tile_ok = ((spots == 1) | (tile_row == 1)) & (target >= 0) & (target < tile_count)
        row_ok = jnp.repeat(tile_ok, TILE)
        past_ok = group - PAST + jnp.arange(PAST, dtype=jnp.int32) >= 0
        key_ok = jnp.concatenate([row_ok, (past_ok[:, None] & row_ok[None, :]).reshape(-1)])
        key_rows = jnp.concatenate([own_keys, past_keys]).reshape(-1, HEADS, HEAD)
        value_rows = jnp.concatenate([own_values, past_values]).reshape(-1, HEADS, HEAD)
        scores = jnp.einsum('qhd,khd->hqk', query_rows.astype(jnp.float32), key_rows.astype(jnp.float32)) * score_scale
        filled = jnp.where(key_ok[None, None, :], scores, -1e+30)
        row_peak = lax.optimization_barrier(jnp.max(filled, axis=-1))
        weights = jnp.where(key_ok[None, None, :], jnp.exp(filled - row_peak[..., None]), 0.0)
        total = lax.optimization_barrier(jnp.sum(weights, axis=-1))
        numer = jnp.einsum('hqk,khd->hqd', weights.astype(jnp.bfloat16).astype(jnp.float32), value_rows.astype(jnp.float32))
        attended = numer / total[..., None]
        return attended.transpose(1, 0, 2).reshape(TILE, D).astype(jnp.bfloat16)
    attended = lax.map(one_tile, jnp.arange(group_count * tile_count, dtype=jnp.int32))
    attended = attended.reshape(group_count * token_count, D)
    projected = jnp.dot(attended, out_weight, preferred_element_type=jnp.float32).reshape(group_count, token_count, D)
    gate_rows = step_gate[noise_step]
    return (gate_rows[:, None, :] * projected).astype(jnp.bfloat16)
```

```python
import functools
import math

import jax
import jax.numpy as jnp
from jax import lax
from jax.experimental import pallas as pl
from jax.experimental.pallas import tpu as pltpu
from jax.sharding import PartitionSpec as P

HEAD = 128
TILE = 128
PAST = 3
SLOTS = PAST + 1
CHUNKS = 4
LOW = -1e30
RATE = math.log2(math.e) / math.sqrt(HEAD)
MESH = pl.DeviceIdType.MESH


def kernel(
    groups, spaces,
    q_hbm, kn_hbm, vn_hbm, kc_hbm, vc_hbm, w_hbm, gate_ref, noise_ref, mask_ref,
    out_ref,
    qbuf, kv, wbuf, own_o, own_st, send_o, send_st, got_o, got_st,
    local_sem, q_send, q_recv, kv_recv, a_send, b_send, f_send, o_send, o_recv, st_send, st_recv,
):
    c = lax.axis_index("tm")
    s = lax.axis_index("space")
    parity = lax.rem(c, 2)
    width = q_hbm.shape[1]
    span = width // CHUNKS
    heads = span // HEAD
    cleans = (kc_hbm, vc_hbm)

    locals_ = [
        pltpu.make_async_copy(q_hbm, qbuf.at[pl.ds(TILE, TILE)], local_sem.at[0]),
        pltpu.make_async_copy(kn_hbm, kv.at[0, pl.ds(0, TILE)], local_sem.at[1]),
        pltpu.make_async_copy(vn_hbm, kv.at[1, pl.ds(0, TILE)], local_sem.at[2]),
        pltpu.make_async_copy(w_hbm, wbuf, local_sem.at[3]),
    ]
    for copy in locals_:
        copy.start()

    sibling = c + 1 - 2 * parity
    far = c - 3 + 6 * parity
    partners = [
        (None, {"tm": sibling}),
        (c >= 2, {"tm": c - 2}),
        (c + 2 < groups, {"tm": c + 2}),
        ((far >= 0) & (far < groups), {"tm": far}),
        (s >= 1, {"space": s - 1}),
        (s + 1 < spaces, {"space": s + 1}),
    ]
    barrier = pltpu.get_barrier_semaphore()
    for valid, where in partners:
        def greet(where=where):
            pl.semaphore_signal(barrier, inc=1, device_id=where, device_id_type=MESH)
        if valid is None:
            greet()
        else:
            pl.when(valid)(greet)
    count = 1
    for valid, _ in partners[1:]:
        count = count + valid.astype(jnp.int32)
    pl.semaphore_wait(barrier, count)

    def columns(j):
        return pl.ds(pl.multiple_of(j * span, span), span)

    def remote(src, dst, send, recv, where):
        return pltpu.make_async_remote_copy(
            src_ref=src, dst_ref=dst, send_sem=send, recv_sem=recv,
            device_id=where, device_id_type=MESH,
        )

    def slot_rows(slot):
        return pl.ds(pl.multiple_of(slot * TILE, TILE), TILE)

    side_ok = (s >= 1, s + 1 < spaces)
    side_id = ({"space": s - 1}, {"space": s + 1})

    def q_copy(side, j):
        other = 1 - side
        return remote(
            q_hbm.at[:, columns(j)],
            qbuf.at[pl.ds(other * 2 * TILE, TILE), columns(j)],
            q_send.at[side, j], q_recv.at[other, j], side_id[side],
        )

    def q_wait(side, j):
        remote(
            q_hbm.at[:, columns(j)],
            qbuf.at[pl.ds(side * 2 * TILE, TILE), columns(j)],
            q_send.at[side, j], q_recv.at[side, j], side_id[side],
        ).wait_recv()

    to_b = c + 1 + 2 * parity
    slot_b = 1 + 2 * parity
    slot_f = 3 - 2 * parity
    a_ok = c + 2 < groups
    b_ok = to_b < groups
    f_ok = c >= 2

    def a_copy(t, j):
        return remote(
            cleans[t].at[:, columns(j)], kv.at[t, pl.ds(2 * TILE, TILE), columns(j)],
            a_send.at[t, j], kv_recv.at[1, t, j], {"tm": c + 2},
        )

    def b_copy(t, j):
        return remote(
            cleans[t].at[:, columns(j)], kv.at[t, slot_rows(slot_b), columns(j)],
            b_send.at[t, j], kv_recv.at[slot_b - 1, t, j], {"tm": to_b},
        )

    def f_copy(t, j):
        return remote(
            kv.at[t, pl.ds(2 * TILE, TILE), columns(j)], kv.at[t, slot_rows(slot_f), columns(j)],
            f_send.at[t, j], kv_recv.at[slot_f - 1, t, j], {"tm": sibling},
        )

    def kv_wait(slot, t, j):
        remote(
            cleans[t].at[:, columns(j)], kv.at[t, pl.ds(slot * TILE, TILE), columns(j)],
            a_send.at[t, j], kv_recv.at[slot - 1, t, j], {"tm": sibling},
        ).wait_recv()

    def o_rows(j):
        return pl.ds(pl.multiple_of(j * span, span), span)

    def o_copies(side, j):
        other = 1 - side
        return (
            remote(
                send_o.at[side, o_rows(j)], got_o.at[other, o_rows(j)],
                o_send.at[side, j], o_recv.at[other, j], side_id[side],
            ),
            remote(
                send_st.at[side, j], got_st.at[other, j],
                st_send.at[side, j], st_recv.at[other, j], side_id[side],
            ),
        )

    def o_wait(side, j):
        remote(
            send_o.at[side, o_rows(j)], got_o.at[side, o_rows(j)],
            o_send.at[side, j], o_recv.at[side, j], side_id[side],
        ).wait_recv()
        remote(
            send_st.at[side, j], got_st.at[side, j],
            st_send.at[side, j], st_recv.at[side, j], side_id[side],
        ).wait_recv()

    def send_all(j, carry):
        @pl.when(a_ok)
        def _():
            for t in range(2):
                a_copy(t, j).start()

        @pl.when(b_ok)
        def _():
            for t in range(2):
                b_copy(t, j).start()

        for side in range(2):
            @pl.when(side_ok[side])
            def _():
                q_copy(side, j).start()
        return carry

    lax.fori_loop(0, CHUNKS, send_all, 0)

    for slot in range(1, SLOTS):
        @pl.when(c < slot)
        def _():
            kv[:, slot * TILE:(slot + 1) * TILE, :] = jnp.zeros((2, TILE, width), kv.dtype)
    for side in range(2):
        @pl.when(jnp.logical_not(side_ok[side]))
        def _():
            qbuf[side * 2 * TILE:side * 2 * TILE + TILE, :] = jnp.zeros((TILE, width), qbuf.dtype)
            got_o[side] = jnp.zeros(got_o.shape[1:], got_o.dtype)
            got_st[side] = jnp.zeros(got_st.shape[1:], got_st.dtype)

    for copy in locals_[:3]:
        copy.wait()

    bias = [None] + [jnp.where(c >= d, 0.0, LOW).astype(jnp.float32) for d in range(1, SLOTS)]

    def attend(j, carry):
        @pl.when(f_ok)
        def _():
            for t in range(2):
                kv_wait(2, t, j)
                f_copy(t, j).start()

        for side in range(2):
            @pl.when(side_ok[side])
            def _():
                q_wait(side, j)

        for slot in (1, 3):
            @pl.when(c >= slot)
            def _():
                for t in range(2):
                    kv_wait(slot, t, j)

        peaks, sums = [], []
        for h in range(heads):
            at = pl.multiple_of(j * span + h * HEAD, HEAD)
            q = qbuf[:, pl.ds(at, HEAD)]
            scores = []
            peak = None
            for d in range(SLOTS):
                k = kv[0, d * TILE:(d + 1) * TILE, pl.ds(at, HEAD)]
                part = lax.dot_general(
                    k, q, (((1,), (1,)), ((), ())), preferred_element_type=jnp.float32
                )
                top = jnp.max(part, axis=0, keepdims=True) * RATE
                if d > 0:
                    top = top + bias[d]
                peak = top if peak is None else jnp.maximum(peak, top)
                scores.append(part)
            total = None
            weights = []
            for d in range(SLOTS):
                shift = -peak if d == 0 else bias[d] - peak
                weight = jnp.exp2(scores[d] * RATE + shift)
                part = jnp.sum(weight, axis=0, keepdims=True)
                total = part if total is None else total + part
                weights.append(weight.astype(jnp.bfloat16))
            v = kv[1, :, pl.ds(at, HEAD)]
            numer = jnp.dot(
                v.T, jnp.concatenate(weights, axis=0), preferred_element_type=jnp.float32
            )
            rows = pl.ds(at, HEAD)
            own_o[rows, :] = numer[:, TILE:2 * TILE]
            send_o[0, rows, :] = numer[:, :TILE].astype(jnp.bfloat16)
            send_o[1, rows, :] = numer[:, 2 * TILE:].astype(jnp.bfloat16)
            peaks.append(peak)
            sums.append(total)
        filler = [jnp.zeros((8 - 2 * heads, 3 * TILE), jnp.float32)]
        stats = jnp.concatenate(peaks + sums + filler, axis=0)
        own_st[j] = stats[:, TILE:2 * TILE]
        send_st[0, j] = stats[:, :TILE]
        send_st[1, j] = stats[:, 2 * TILE:]
        for side in range(2):
            @pl.when(side_ok[side])
            def _():
                for copy in o_copies(side, j):
                    copy.start()
        return carry

    lax.fori_loop(0, CHUNKS, attend, 0)

    locals_[3].wait()
    allowed = (
        side_ok[0] & (mask_ref[0] == 1),
        side_ok[1] & (mask_ref[2] == 1),
    )
    noise = noise_ref[0]
    gate = gate_ref[0:1, :]
    for level in range(1, gate_ref.shape[0]):
        gate = jnp.where(noise == level, gate_ref[level:level + 1, :], gate)

    projected = jnp.zeros((TILE, wbuf.shape[1]), jnp.float32)
    for j in range(CHUNKS):
        for side in range(2):
            @pl.when(side_ok[side])
            def _():
                o_wait(side, j)
        merged = []
        for h in range(heads):
            rows = slice(j * span + h * HEAD, j * span + (h + 1) * HEAD)
            mine = own_st[j, h:h + 1, :]
            tops = [
                jnp.where(allowed[side], got_st[side, j, h:h + 1, :], LOW) for side in range(2)
            ]
            peak = jnp.maximum(mine, jnp.maximum(tops[0], tops[1]))
            factor = jnp.exp2(mine - peak)
            total = factor * own_st[j, heads + h:heads + h + 1, :]
            numer = factor * own_o[rows, :]
            for side in range(2):
                factor = jnp.exp2(tops[side] - peak)
                total = total + factor * got_st[side, j, heads + h:heads + h + 1, :]
                numer = numer + factor * got_o[side, rows, :].astype(jnp.float32)
            merged.append((numer / total).T.astype(jnp.bfloat16))
        projected = projected + jnp.dot(
            jnp.concatenate(merged, axis=1), wbuf[j * span:(j + 1) * span, :],
            preferred_element_type=jnp.float32,
        )
    out_ref[...] = (gate * projected).astype(out_ref.dtype)

    def drain(j, carry):
        @pl.when(a_ok)
        def _():
            for t in range(2):
                a_copy(t, j).wait_send()

        @pl.when(b_ok)
        def _():
            for t in range(2):
                b_copy(t, j).wait_send()

        @pl.when(f_ok)
        def _():
            for t in range(2):
                f_copy(t, j).wait_send()

        for side in range(2):
            @pl.when(side_ok[side])
            def _():
                q_copy(side, j).wait_send()
                for copy in o_copies(side, j):
                    copy.wait_send()
        return carry

    lax.fori_loop(0, CHUNKS, drain, 0)


def on_device(
    groups, spaces,
    query, key_new, value_new, key_clean, value_clean, out_weight, step_gate, noise_step, tile_mask,
):
    width = query.shape[2]
    anywhere = pl.BlockSpec(memory_space=pl.ANY)
    vmem = pl.BlockSpec(memory_space=pltpu.VMEM)
    smem = pl.BlockSpec(memory_space=pltpu.SMEM)
    dma = pltpu.SemaphoreType.DMA
    out = pl.pallas_call(
        functools.partial(kernel, groups, spaces),
        out_shape=jax.ShapeDtypeStruct((TILE, out_weight.shape[1]), jnp.bfloat16),
        in_specs=[anywhere] * 6 + [vmem, smem, smem],
        out_specs=vmem,
        scratch_shapes=[
            pltpu.VMEM((3 * TILE, width), jnp.bfloat16),
            pltpu.VMEM((2, SLOTS * TILE, width), jnp.bfloat16),
            pltpu.VMEM(out_weight.shape, jnp.bfloat16),
            pltpu.VMEM((width, TILE), jnp.float32),
            pltpu.VMEM((CHUNKS, 8, TILE), jnp.float32),
            pltpu.VMEM((2, width, TILE), jnp.bfloat16),
            pltpu.VMEM((2, CHUNKS, 8, TILE), jnp.float32),
            pltpu.VMEM((2, width, TILE), jnp.bfloat16),
            pltpu.VMEM((2, CHUNKS, 8, TILE), jnp.float32),
            dma((4,)),
            dma((2, CHUNKS)), dma((2, CHUNKS)),
            dma((PAST, 2, CHUNKS)),
            dma((2, CHUNKS)), dma((2, CHUNKS)), dma((2, CHUNKS)),
            dma((2, CHUNKS)), dma((2, CHUNKS)),
            dma((2, CHUNKS)), dma((2, CHUNKS)),
        ],
        compiler_params=pltpu.CompilerParams(
            collective_id=0, has_side_effects=True, vmem_limit_bytes=56 * 2**20
        ),
        name="tile_attention",
    )(
        query[0], key_new[0], value_new[0], key_clean[0], value_clean[0], out_weight,
        step_gate, noise_step, tile_mask.reshape(-1),
    )
    return out[None]


def solution(mesh):
    split = P("tm", "space", None)
    placed = (split, split, split, split, split, P(), P(), P("tm"), split)
    return jax.shard_map(
        functools.partial(on_device, mesh.shape["tm"], mesh.shape["space"]),
        mesh=mesh, in_specs=placed, out_specs=split, check_vma=False,
    )
```

```python
import functools
import math

import jax
import jax.numpy as jnp
from jax import lax
from jax.experimental import pallas as pl
from jax.experimental.pallas import tpu as pltpu
from jax.sharding import PartitionSpec as P

HEAD = 128
TILE = 128
PAST = 3
SLOTS = PAST + 1
CHUNKS = 6
AHEAD = 2
LOW = -1e30
RATE = math.log2(math.e) / math.sqrt(HEAD)
MESH = pl.DeviceIdType.MESH


def kernel(
    groups, spaces,
    q_hbm, kn_hbm, vn_hbm, kc_hbm, vc_hbm, w_hbm, gate_ref, noise_ref, mask_ref,
    out_ref,
    qbuf, kv, wbuf, own_o, own_st, send_o, send_st, got_o, got_st,
    local_sem, q_send, q_recv, kv_recv, a_send, b_send, f_send, r_send, o_send, o_recv, st_send, st_recv,
):
    c = lax.axis_index("tm")
    s = lax.axis_index("space")
    parity = lax.rem(c, 2)
    width = q_hbm.shape[1]
    span = width // CHUNKS
    heads = span // HEAD
    cleans = (kc_hbm, vc_hbm)

    locals_ = [
        pltpu.make_async_copy(q_hbm, qbuf.at[pl.ds(TILE, TILE)], local_sem.at[0]),
        pltpu.make_async_copy(kn_hbm, kv.at[0, pl.ds(0, TILE)], local_sem.at[1]),
        pltpu.make_async_copy(vn_hbm, kv.at[1, pl.ds(0, TILE)], local_sem.at[2]),
        pltpu.make_async_copy(w_hbm, wbuf, local_sem.at[3]),
    ]
    for copy in locals_:
        copy.start()

    sibling = c + 1 - 2 * parity
    far = c - 3 + 6 * parity
    corner = lax.rem(c, 4)
    a_ok = (c + 2 < groups) & jnp.logical_not((corner == 3) & (c + 3 < groups))
    relay_ok = (corner == 2) & (c >= 3)
    relayed = (corner == 1) & (c >= 2) & (c + 1 < groups)
    partners = [
        (None, {"tm": sibling}),
        ((c >= 2) & jnp.logical_not(relayed), {"tm": c - 2}),
        (a_ok, {"tm": c + 2}),
        (relay_ok, {"tm": c - 1}),
        (relayed, {"tm": c + 1}),
        ((far >= 0) & (far < groups), {"tm": far}),
        (s >= 1, {"space": s - 1}),
        (s + 1 < spaces, {"space": s + 1}),
    ]
    barrier = pltpu.get_barrier_semaphore()
    for valid, where in partners:
        def greet(where=where):
            pl.semaphore_signal(barrier, inc=1, device_id=where, device_id_type=MESH)
        if valid is None:
            greet()
        else:
            pl.when(valid)(greet)
    count = 1
    for valid, _ in partners[1:]:
        count = count + valid.astype(jnp.int32)
    pl.semaphore_wait(barrier, count)

    def columns(j):
        return pl.ds(pl.multiple_of(j * span, span), span)

    def remote(src, dst, send, recv, where):
        return pltpu.make_async_remote_copy(
            src_ref=src, dst_ref=dst, send_sem=send, recv_sem=recv,
            device_id=where, device_id_type=MESH,
        )

    def slot_rows(slot):
        return pl.ds(pl.multiple_of(slot * TILE, TILE), TILE)

    side_ok = (s >= 1, s + 1 < spaces)
    side_id = ({"space": s - 1}, {"space": s + 1})

    def q_copy(side, j):
        other = 1 - side
        return remote(
            q_hbm.at[:, columns(j)],
            qbuf.at[pl.ds(other * 2 * TILE, TILE), columns(j)],
            q_send.at[side, j], q_recv.at[other, j], side_id[side],
        )

    def q_wait(side, j):
        remote(
            q_hbm.at[:, columns(j)],
            qbuf.at[pl.ds(side * 2 * TILE, TILE), columns(j)],
            q_send.at[side, j], q_recv.at[side, j], side_id[side],
        ).wait_recv()

    to_b = c + 1 + 2 * parity
    slot_b = 1 + 2 * parity
    slot_f = 3 - 2 * parity
    b_ok = to_b < groups
    f_ok = c >= 2

    def a_copy(t, j):
        return remote(
            cleans[t].at[:, columns(j)], kv.at[t, pl.ds(2 * TILE, TILE), columns(j)],
            a_send.at[t, j], kv_recv.at[1, t, j], {"tm": c + 2},
        )

    def b_copy(t, j):
        return remote(
            cleans[t].at[:, columns(j)], kv.at[t, slot_rows(slot_b), columns(j)],
            b_send.at[t, j], kv_recv.at[slot_b - 1, t, j], {"tm": to_b},
        )

    def f_copy(t, j):
        return remote(
            kv.at[t, pl.ds(2 * TILE, TILE), columns(j)], kv.at[t, slot_rows(slot_f), columns(j)],
            f_send.at[t, j], kv_recv.at[slot_f - 1, t, j], {"tm": sibling},
        )

    def r_copy(t, j):
        return remote(
            kv.at[t, pl.ds(3 * TILE, TILE), columns(j)], kv.at[t, pl.ds(2 * TILE, TILE), columns(j)],
            r_send.at[t, j], kv_recv.at[1, t, j], {"tm": c - 1},
        )

    def kv_wait(slot, t, j):
        remote(
            cleans[t].at[:, columns(j)], kv.at[t, pl.ds(slot * TILE, TILE), columns(j)],
            a_send.at[t, j], kv_recv.at[slot - 1, t, j], {"tm": sibling},
        ).wait_recv()

    def o_rows(j):
        return pl.ds(pl.multiple_of(j * span, span), span)

    def o_copies(side, j):
        other = 1 - side
        return (
            remote(
                send_o.at[side, o_rows(j)], got_o.at[other, o_rows(j)],
                o_send.at[side, j], o_recv.at[other, j], side_id[side],
            ),
            remote(
                send_st.at[side, j], got_st.at[other, j],
                st_send.at[side, j], st_recv.at[other, j], side_id[side],
            ),
        )

    def o_wait(side, j):
        remote(
            send_o.at[side, o_rows(j)], got_o.at[side, o_rows(j)],
            o_send.at[side, j], o_recv.at[side, j], side_id[side],
        ).wait_recv()
        remote(
            send_st.at[side, j], got_st.at[side, j],
            st_send.at[side, j], st_recv.at[side, j], side_id[side],
        ).wait_recv()

    def start_sends(j):
        @pl.when(a_ok)
        def _():
            for t in range(2):
                a_copy(t, j).start()

        @pl.when(b_ok)
        def _():
            for t in range(2):
                b_copy(t, j).start()

        for side in range(2):
            @pl.when(side_ok[side])
            def _():
                q_copy(side, j).start()

    def wait_sends(j):
        @pl.when(a_ok)
        def _():
            for t in range(2):
                a_copy(t, j).wait_send()

        @pl.when(b_ok)
        def _():
            for t in range(2):
                b_copy(t, j).wait_send()

        for side in range(2):
            @pl.when(side_ok[side])
            def _():
                q_copy(side, j).wait_send()

    for j in range(AHEAD):
        start_sends(j)

    for slot in range(1, SLOTS):
        @pl.when(c < slot)
        def _():
            kv[:, slot * TILE:(slot + 1) * TILE, :] = jnp.zeros((2, TILE, width), kv.dtype)
    for side in range(2):
        @pl.when(jnp.logical_not(side_ok[side]))
        def _():
            qbuf[side * 2 * TILE:side * 2 * TILE + TILE, :] = jnp.zeros((TILE, width), qbuf.dtype)
            got_o[side] = jnp.zeros(got_o.shape[1:], got_o.dtype)
            got_st[side] = jnp.zeros(got_st.shape[1:], got_st.dtype)

    for copy in locals_[:3]:
        copy.wait()

    bias = [None] + [jnp.where(c >= d, 0.0, LOW).astype(jnp.float32) for d in range(1, SLOTS)]

    def attend(j, carry):
        @pl.when(relay_ok)
        def _():
            for t in range(2):
                kv_wait(3, t, j)
                r_copy(t, j).start()

        @pl.when(f_ok)
        def _():
            for t in range(2):
                kv_wait(2, t, j)
                f_copy(t, j).start()

        @pl.when(j + AHEAD < CHUNKS)
        def _():
            wait_sends(j)
            start_sends(j + AHEAD)

        for side in range(2):
            @pl.when(side_ok[side])
            def _():
                q_wait(side, j)

        for slot, awaited in ((1, c >= 1), (3, (c >= 3) & jnp.logical_not(relay_ok))):
            @pl.when(awaited)
            def _():
                for t in range(2):
                    kv_wait(slot, t, j)

        peaks, sums = [], []
        for h in range(heads):
            at = pl.multiple_of(j * span + h * HEAD, HEAD)
            q = qbuf[:, pl.ds(at, HEAD)]
            scores = []
            peak = None
            for d in range(SLOTS):
                k = kv[0, d * TILE:(d + 1) * TILE, pl.ds(at, HEAD)]
                part = lax.dot_general(
                    k, q, (((1,), (1,)), ((), ())), preferred_element_type=jnp.float32
                )
                top = jnp.max(part, axis=0, keepdims=True) * RATE
                if d > 0:
                    top = top + bias[d]
                peak = top if peak is None else jnp.maximum(peak, top)
                scores.append(part)
            total = None
            weights = []
            for d in range(SLOTS):
                shift = -peak if d == 0 else bias[d] - peak
                weight = jnp.exp2(scores[d] * RATE + shift)
                part = jnp.sum(weight, axis=0, keepdims=True)
                total = part if total is None else total + part
                weights.append(weight.astype(jnp.bfloat16))
            v = kv[1, :, pl.ds(at, HEAD)]
            numer = jnp.dot(
                v.T, jnp.concatenate(weights, axis=0), preferred_element_type=jnp.float32
            )
            rows = pl.ds(at, HEAD)
            own_o[rows, :] = numer[:, TILE:2 * TILE]
            send_o[0, rows, :] = numer[:, :TILE].astype(jnp.bfloat16)
            send_o[1, rows, :] = numer[:, 2 * TILE:].astype(jnp.bfloat16)
            peaks.append(peak)
            sums.append(total)
        filler = [jnp.zeros((8 - 2 * heads, 3 * TILE), jnp.float32)]
        stats = jnp.concatenate(peaks + sums + filler, axis=0)
        own_st[j] = stats[:, TILE:2 * TILE]
        send_st[0, j] = stats[:, :TILE]
        send_st[1, j] = stats[:, 2 * TILE:]
        for side in range(2):
            @pl.when(side_ok[side])
            def _():
                for copy in o_copies(side, j):
                    copy.start()
        return carry

    lax.fori_loop(0, CHUNKS, attend, 0)

    locals_[3].wait()
    allowed = (
        side_ok[0] & (mask_ref[0] == 1),
        side_ok[1] & (mask_ref[2] == 1),
    )
    noise = noise_ref[0]
    gate = gate_ref[0:1, :]
    for level in range(1, gate_ref.shape[0]):
        gate = jnp.where(noise == level, gate_ref[level:level + 1, :], gate)

    projected = jnp.zeros((TILE, wbuf.shape[1]), jnp.float32)
    for j in range(CHUNKS):
        for side in range(2):
            @pl.when(side_ok[side])
            def _():
                o_wait(side, j)
        merged = []
        for h in range(heads):
            rows = slice(j * span + h * HEAD, j * span + (h + 1) * HEAD)
            mine = own_st[j, h:h + 1, :]
            tops = [
                jnp.where(allowed[side], got_st[side, j, h:h + 1, :], LOW) for side in range(2)
            ]
            peak = jnp.maximum(mine, jnp.maximum(tops[0], tops[1]))
            factor = jnp.exp2(mine - peak)
            total = factor * own_st[j, heads + h:heads + h + 1, :]
            numer = factor * own_o[rows, :]
            for side in range(2):
                factor = jnp.exp2(tops[side] - peak)
                total = total + factor * got_st[side, j, heads + h:heads + h + 1, :]
                numer = numer + factor * got_o[side, rows, :].astype(jnp.float32)
            merged.append((numer / total).T.astype(jnp.bfloat16))
        projected = projected + jnp.dot(
            jnp.concatenate(merged, axis=1), wbuf[j * span:(j + 1) * span, :],
            preferred_element_type=jnp.float32,
        )
    out_ref[...] = (gate * projected).astype(out_ref.dtype)

    for j in range(CHUNKS - AHEAD, CHUNKS):
        wait_sends(j)

    def drain(j, carry):
        @pl.when(relay_ok)
        def _():
            for t in range(2):
                r_copy(t, j).wait_send()

        @pl.when(f_ok)
        def _():
            for t in range(2):
                f_copy(t, j).wait_send()

        for side in range(2):
            @pl.when(side_ok[side])
            def _():
                for copy in o_copies(side, j):
                    copy.wait_send()
        return carry

    lax.fori_loop(0, CHUNKS, drain, 0)


def on_device(
    groups, spaces,
    query, key_new, value_new, key_clean, value_clean, out_weight, step_gate, noise_step, tile_mask,
):
    width = query.shape[2]
    anywhere = pl.BlockSpec(memory_space=pl.ANY)
    vmem = pl.BlockSpec(memory_space=pltpu.VMEM)
    smem = pl.BlockSpec(memory_space=pltpu.SMEM)
    dma = pltpu.SemaphoreType.DMA
    out = pl.pallas_call(
        functools.partial(kernel, groups, spaces),
        out_shape=jax.ShapeDtypeStruct((TILE, out_weight.shape[1]), jnp.bfloat16),
        in_specs=[anywhere] * 6 + [vmem, smem, smem],
        out_specs=vmem,
        scratch_shapes=[
            pltpu.VMEM((3 * TILE, width), jnp.bfloat16),
            pltpu.VMEM((2, SLOTS * TILE, width), jnp.bfloat16),
            pltpu.VMEM(out_weight.shape, jnp.bfloat16),
            pltpu.VMEM((width, TILE), jnp.float32),
            pltpu.VMEM((CHUNKS, 8, TILE), jnp.float32),
            pltpu.VMEM((2, width, TILE), jnp.bfloat16),
            pltpu.VMEM((2, CHUNKS, 8, TILE), jnp.float32),
            pltpu.VMEM((2, width, TILE), jnp.bfloat16),
            pltpu.VMEM((2, CHUNKS, 8, TILE), jnp.float32),
            dma((4,)),
            dma((2, CHUNKS)), dma((2, CHUNKS)),
            dma((PAST, 2, CHUNKS)),
            dma((2, CHUNKS)), dma((2, CHUNKS)), dma((2, CHUNKS)), dma((2, CHUNKS)),
            dma((2, CHUNKS)), dma((2, CHUNKS)),
            dma((2, CHUNKS)), dma((2, CHUNKS)),
        ],
        compiler_params=pltpu.CompilerParams(
            collective_id=0, has_side_effects=True, vmem_limit_bytes=56 * 2**20
        ),
        name="tile_attention",
    )(
        query[0], key_new[0], value_new[0], key_clean[0], value_clean[0], out_weight,
        step_gate, noise_step, tile_mask.reshape(-1),
    )
    return out[None]


def solution(mesh):
    split = P("tm", "space", None)
    placed = (split, split, split, split, split, P(), P(), P("tm"), split)
    return jax.shard_map(
        functools.partial(on_device, mesh.shape["tm"], mesh.shape["space"]),
        mesh=mesh, in_specs=placed, out_specs=split, check_vma=False,
    )
```

```python
import functools
import math

import jax
import jax.numpy as jnp
from jax import lax
from jax.experimental import pallas as pl
from jax.experimental.pallas import tpu as pltpu
from jax.sharding import PartitionSpec as P

HEAD = 128
TILE = 128
PAST = 3
SLOTS = PAST + 1
CHUNKS = 6
AHEAD = 3
LOW = -1e30
RATE = math.log2(math.e) / math.sqrt(HEAD)
MESH = pl.DeviceIdType.MESH


def kernel(
    groups, spaces,
    q_hbm, kn_hbm, vn_hbm, kc_hbm, vc_hbm, w_hbm, mask_ref,
    out_ref,
    qbuf, kv, wbuf, own_o, own_st, send_o, send_st, got_o, got_st,
    local_sem, q_send, q_recv, kv_recv, a_send, b_send, f_send, r_send, o_send, o_recv, st_send, st_recv,
):
    c = lax.axis_index("tm")
    s = lax.axis_index("space")
    parity = lax.rem(c, 2)
    width = q_hbm.shape[1]
    span = width // CHUNKS
    heads = span // HEAD
    cleans = (kc_hbm, vc_hbm)

    locals_ = [
        pltpu.make_async_copy(q_hbm, qbuf.at[pl.ds(TILE, TILE)], local_sem.at[0]),
        pltpu.make_async_copy(kn_hbm, kv.at[0, pl.ds(0, TILE)], local_sem.at[1]),
        pltpu.make_async_copy(vn_hbm, kv.at[1, pl.ds(0, TILE)], local_sem.at[2]),
        pltpu.make_async_copy(w_hbm, wbuf, local_sem.at[3]),
    ]
    for copy in locals_:
        copy.start()

    sibling = c + 1 - 2 * parity
    far = c - 3 + 6 * parity
    corner = lax.rem(c, 4)
    a_ok = (c + 2 < groups) & jnp.logical_not((corner == 3) & (c + 3 < groups))
    relay_ok = (corner == 2) & (c >= 3)
    relayed = (corner == 1) & (c >= 2) & (c + 1 < groups)
    partners = [
        (None, {"tm": sibling}),
        ((c >= 2) & jnp.logical_not(relayed), {"tm": c - 2}),
        (a_ok, {"tm": c + 2}),
        (relay_ok, {"tm": c - 1}),
        (relayed, {"tm": c + 1}),
        ((far >= 0) & (far < groups), {"tm": far}),
        (s >= 1, {"space": s - 1}),
        (s + 1 < spaces, {"space": s + 1}),
    ]
    barrier = pltpu.get_barrier_semaphore()
    for valid, where in partners:
        def greet(where=where):
            pl.semaphore_signal(barrier, inc=1, device_id=where, device_id_type=MESH)
        if valid is None:
            greet()
        else:
            pl.when(valid)(greet)
    count = 1
    for valid, _ in partners[1:]:
        count = count + valid.astype(jnp.int32)
    pl.semaphore_wait(barrier, count)

    def columns(j):
        return pl.ds(pl.multiple_of(j * span, span), span)

    def remote(src, dst, send, recv, where):
        return pltpu.make_async_remote_copy(
            src_ref=src, dst_ref=dst, send_sem=send, recv_sem=recv,
            device_id=where, device_id_type=MESH,
        )

    def slot_rows(slot):
        return pl.ds(pl.multiple_of(slot * TILE, TILE), TILE)

    side_ok = (s >= 1, s + 1 < spaces)
    side_id = ({"space": s - 1}, {"space": s + 1})

    def q_copy(side, j):
        other = 1 - side
        return remote(
            q_hbm.at[:, columns(j)],
            qbuf.at[pl.ds(other * 2 * TILE, TILE), columns(j)],
            q_send.at[side, j], q_recv.at[other, j], side_id[side],
        )

    def q_wait(side, j):
        remote(
            q_hbm.at[:, columns(j)],
            qbuf.at[pl.ds(side * 2 * TILE, TILE), columns(j)],
            q_send.at[side, j], q_recv.at[side, j], side_id[side],
        ).wait_recv()

    to_b = c + 1 + 2 * parity
    slot_b = 1 + 2 * parity
    slot_f = 3 - 2 * parity
    b_ok = to_b < groups
    f_ok = c >= 2

    def a_copy(t, j):
        return remote(
            cleans[t].at[:, columns(j)], kv.at[t, pl.ds(2 * TILE, TILE), columns(j)],
            a_send.at[t, j], kv_recv.at[1, t, j], {"tm": c + 2},
        )

    def b_copy(t, j):
        return remote(
            cleans[t].at[:, columns(j)], kv.at[t, slot_rows(slot_b), columns(j)],
            b_send.at[t, j], kv_recv.at[slot_b - 1, t, j], {"tm": to_b},
        )

    def f_copy(t, j):
        return remote(
            kv.at[t, pl.ds(2 * TILE, TILE), columns(j)], kv.at[t, slot_rows(slot_f), columns(j)],
            f_send.at[t, j], kv_recv.at[slot_f - 1, t, j], {"tm": sibling},
        )

    def r_copy(t, j):
        return remote(
            kv.at[t, pl.ds(3 * TILE, TILE), columns(j)], kv.at[t, pl.ds(2 * TILE, TILE), columns(j)],
            r_send.at[t, j], kv_recv.at[1, t, j], {"tm": c - 1},
        )

    def kv_wait(slot, t, j):
        remote(
            cleans[t].at[:, columns(j)], kv.at[t, pl.ds(slot * TILE, TILE), columns(j)],
            a_send.at[t, j], kv_recv.at[slot - 1, t, j], {"tm": sibling},
        ).wait_recv()

    def o_rows(j):
        return pl.ds(pl.multiple_of(j * span, span), span)

    def o_copies(side, j):
        other = 1 - side
        return (
            remote(
                send_o.at[side, o_rows(j)], got_o.at[other, o_rows(j)],
                o_send.at[side, j], o_recv.at[other, j], side_id[side],
            ),
            remote(
                send_st.at[side, j], got_st.at[other, j],
                st_send.at[side, j], st_recv.at[other, j], side_id[side],
            ),
        )

    def o_wait(side, j):
        remote(
            send_o.at[side, o_rows(j)], got_o.at[side, o_rows(j)],
            o_send.at[side, j], o_recv.at[side, j], side_id[side],
        ).wait_recv()
        remote(
            send_st.at[side, j], got_st.at[side, j],
            st_send.at[side, j], st_recv.at[side, j], side_id[side],
        ).wait_recv()

    def start_sends(j):
        @pl.when(a_ok)
        def _():
            for t in range(2):
                a_copy(t, j).start()

        for side in range(2):
            @pl.when(side_ok[side])
            def _():
                q_copy(side, j).start()

    def wait_sends(j):
        @pl.when(a_ok)
        def _():
            for t in range(2):
                a_copy(t, j).wait_send()

        for side in range(2):
            @pl.when(side_ok[side])
            def _():
                q_copy(side, j).wait_send()

    for j in range(CHUNKS):
        @pl.when(b_ok)
        def _():
            for t in range(2):
                b_copy(t, j).start()

        if j < AHEAD:
            start_sends(j)

    for slot in range(1, SLOTS):
        @pl.when(c < slot)
        def _():
            kv[:, slot * TILE:(slot + 1) * TILE, :] = jnp.zeros((2, TILE, width), kv.dtype)
    for side in range(2):
        @pl.when(jnp.logical_not(side_ok[side]))
        def _():
            qbuf[side * 2 * TILE:side * 2 * TILE + TILE, :] = jnp.zeros((TILE, width), qbuf.dtype)
            got_o[side] = jnp.zeros(got_o.shape[1:], got_o.dtype)
            got_st[side] = jnp.zeros(got_st.shape[1:], got_st.dtype)

    for copy in locals_[:3]:
        copy.wait()

    bias = [None] + [jnp.where(c >= d, 0.0, LOW).astype(jnp.float32) for d in range(1, SLOTS)]

    def attend(j, carry):
        @pl.when(relay_ok)
        def _():
            for t in range(2):
                kv_wait(3, t, j)
                r_copy(t, j).start()

        @pl.when(j + AHEAD < CHUNKS)
        def _():
            wait_sends(j)
            start_sends(j + AHEAD)

        @pl.when(f_ok)
        def _():
            for t in range(2):
                kv_wait(2, t, j)
                f_copy(t, j).start()

        for side in range(2):
            @pl.when(side_ok[side])
            def _():
                q_wait(side, j)

        for slot, awaited in ((1, c >= 1), (3, (c >= 3) & jnp.logical_not(relay_ok))):
            @pl.when(awaited)
            def _():
                for t in range(2):
                    kv_wait(slot, t, j)

        peaks, sums = [], []
        for h in range(heads):
            at = pl.multiple_of(j * span + h * HEAD, HEAD)
            q = qbuf[:, pl.ds(at, HEAD)]
            scores = []
            peak = None
            for d in range(SLOTS):
                k = kv[0, d * TILE:(d + 1) * TILE, pl.ds(at, HEAD)]
                part = lax.dot_general(
                    k, q, (((1,), (1,)), ((), ())), preferred_element_type=jnp.float32
                )
                top = jnp.max(part, axis=0, keepdims=True) * RATE
                if d > 0:
                    top = top + bias[d]
                peak = top if peak is None else jnp.maximum(peak, top)
                scores.append(part)
            total = None
            weights = []
            for d in range(SLOTS):
                shift = -peak if d == 0 else bias[d] - peak
                weight = jnp.exp2(scores[d] * RATE + shift)
                part = jnp.sum(weight, axis=0, keepdims=True)
                total = part if total is None else total + part
                weights.append(weight.astype(jnp.bfloat16))
            v = kv[1, :, pl.ds(at, HEAD)]
            numer = jnp.dot(
                v.T, jnp.concatenate(weights, axis=0), preferred_element_type=jnp.float32
            )
            rows = pl.ds(at, HEAD)
            own_o[rows, :] = numer[:, TILE:2 * TILE]
            send_o[0, rows, :] = numer[:, :TILE].astype(jnp.bfloat16)
            send_o[1, rows, :] = numer[:, 2 * TILE:].astype(jnp.bfloat16)
            peaks.append(peak)
            sums.append(total)
        filler = [jnp.zeros((8 - 2 * heads, 3 * TILE), jnp.float32)]
        stats = jnp.concatenate(peaks + sums + filler, axis=0)
        own_st[j] = stats[:, TILE:2 * TILE]
        send_st[0, j] = stats[:, :TILE]
        send_st[1, j] = stats[:, 2 * TILE:]
        for side in range(2):
            @pl.when(side_ok[side])
            def _():
                for copy in o_copies(side, j):
                    copy.start()
        return carry

    lax.fori_loop(0, CHUNKS, attend, 0)

    locals_[3].wait()
    allowed = (
        side_ok[0] & (mask_ref[0] == 1),
        side_ok[1] & (mask_ref[2] == 1),
    )
    projected = jnp.zeros((TILE, wbuf.shape[1]), jnp.float32)
    for j in range(CHUNKS):
        for side in range(2):
            @pl.when(side_ok[side])
            def _():
                o_wait(side, j)
        merged = []
        for h in range(heads):
            rows = slice(j * span + h * HEAD, j * span + (h + 1) * HEAD)
            mine = own_st[j, h:h + 1, :]
            tops = [
                jnp.where(allowed[side], got_st[side, j, h:h + 1, :], LOW) for side in range(2)
            ]
            peak = jnp.maximum(mine, jnp.maximum(tops[0], tops[1]))
            factor = jnp.exp2(mine - peak)
            total = factor * own_st[j, heads + h:heads + h + 1, :]
            numer = factor * own_o[rows, :]
            for side in range(2):
                factor = jnp.exp2(tops[side] - peak)
                total = total + factor * got_st[side, j, heads + h:heads + h + 1, :]
                numer = numer + factor * got_o[side, rows, :].astype(jnp.float32)
            merged.append((numer / total).T.astype(jnp.bfloat16))
        projected = projected + jnp.dot(
            jnp.concatenate(merged, axis=1), wbuf[j * span:(j + 1) * span, :],
            preferred_element_type=jnp.float32,
        )
    out_ref[...] = projected

    for j in range(CHUNKS - AHEAD, CHUNKS):
        wait_sends(j)

    def drain(j, carry):
        @pl.when(relay_ok)
        def _():
            for t in range(2):
                r_copy(t, j).wait_send()

        @pl.when(b_ok)
        def _():
            for t in range(2):
                b_copy(t, j).wait_send()

        @pl.when(f_ok)
        def _():
            for t in range(2):
                f_copy(t, j).wait_send()

        for side in range(2):
            @pl.when(side_ok[side])
            def _():
                for copy in o_copies(side, j):
                    copy.wait_send()
        return carry

    lax.fori_loop(0, CHUNKS, drain, 0)


def on_device(
    groups, spaces,
    query, key_new, value_new, key_clean, value_clean, out_weight, step_gate, noise_step, tile_mask,
):
    width = query.shape[2]
    anywhere = pl.BlockSpec(memory_space=pl.ANY)
    vmem = pl.BlockSpec(memory_space=pltpu.VMEM)
    smem = pl.BlockSpec(memory_space=pltpu.SMEM)
    dma = pltpu.SemaphoreType.DMA
    projected = pl.pallas_call(
        functools.partial(kernel, groups, spaces),
        out_shape=jax.ShapeDtypeStruct((TILE, out_weight.shape[1]), jnp.float32),
        in_specs=[anywhere] * 6 + [smem],
        out_specs=vmem,
        scratch_shapes=[
            pltpu.VMEM((3 * TILE, width), jnp.bfloat16),
            pltpu.VMEM((2, SLOTS * TILE, width), jnp.bfloat16),
            pltpu.VMEM(out_weight.shape, jnp.bfloat16),
            pltpu.VMEM((width, TILE), jnp.float32),
            pltpu.VMEM((CHUNKS, 8, TILE), jnp.float32),
            pltpu.VMEM((2, width, TILE), jnp.bfloat16),
            pltpu.VMEM((2, CHUNKS, 8, TILE), jnp.float32),
            pltpu.VMEM((2, width, TILE), jnp.bfloat16),
            pltpu.VMEM((2, CHUNKS, 8, TILE), jnp.float32),
            dma((4,)),
            dma((2, CHUNKS)), dma((2, CHUNKS)),
            dma((PAST, 2, CHUNKS)),
            dma((2, CHUNKS)), dma((2, CHUNKS)), dma((2, CHUNKS)), dma((2, CHUNKS)),
            dma((2, CHUNKS)), dma((2, CHUNKS)),
            dma((2, CHUNKS)), dma((2, CHUNKS)),
        ],
        compiler_params=pltpu.CompilerParams(
            collective_id=0, has_side_effects=True, vmem_limit_bytes=56 * 2**20
        ),
        name="tile_attention",
    )(
        query[0], key_new[0], value_new[0], key_clean[0], value_clean[0], out_weight,
        tile_mask.reshape(-1),
    )
    gate = lax.dynamic_slice_in_dim(step_gate, noise_step[0], 1, axis=0)
    return (gate * projected).astype(jnp.bfloat16)[None]


def solution(mesh):
    split = P("tm", "space", None)
    placed = (split, split, split, split, split, P(), P(), P("tm"), split)
    return jax.shard_map(
        functools.partial(on_device, mesh.shape["tm"], mesh.shape["space"]),
        mesh=mesh, in_specs=placed, out_specs=split, check_vma=False,
    )
```

```python
import functools
import math

import jax
import jax.numpy as jnp
from jax import lax
from jax.experimental import pallas as pl
from jax.experimental.pallas import tpu as pltpu
from jax.sharding import PartitionSpec as P

HEAD = 128
TILE = 128
PAST = 3
SLOTS = PAST + 1
CHUNKS = 6
AHEAD = 3
LOW = -1e30
RATE = math.log2(math.e) / math.sqrt(HEAD)
MESH = pl.DeviceIdType.MESH


def kernel(
    groups, spaces,
    q_hbm, kn_hbm, vn_hbm, kc_hbm, vc_hbm, w_hbm, gate_ref, noise_ref, mask_ref,
    out_ref,
    qbuf, kv, wbuf, own_o, own_st, send_o, send_st, got_o, got_st,
    local_sem, q_send, q_recv, kv_recv, a_send, b_send, f_send, r_send, o_send, o_recv, st_send, st_recv,
):
    c = lax.axis_index("tm")
    s = lax.axis_index("space")
    parity = lax.rem(c, 2)
    width = q_hbm.shape[1]
    span = width // CHUNKS
    heads = span // HEAD
    cleans = (kc_hbm, vc_hbm)

    locals_ = [
        pltpu.make_async_copy(q_hbm, qbuf.at[pl.ds(TILE, TILE)], local_sem.at[0]),
        pltpu.make_async_copy(kn_hbm, kv.at[0, pl.ds(0, TILE)], local_sem.at[1]),
        pltpu.make_async_copy(vn_hbm, kv.at[1, pl.ds(0, TILE)], local_sem.at[2]),
        pltpu.make_async_copy(w_hbm, wbuf, local_sem.at[3]),
    ]
    for copy in locals_:
        copy.start()

    sibling = c + 1 - 2 * parity
    far = c - 3 + 6 * parity
    corner = lax.rem(c, 4)
    a_ok = (c + 2 < groups) & jnp.logical_not((corner == 3) & (c + 3 < groups))
    relay_ok = (corner == 2) & (c >= 3)
    relayed = (corner == 1) & (c >= 2) & (c + 1 < groups)
    partners = [
        (None, {"tm": sibling}),
        ((c >= 2) & jnp.logical_not(relayed), {"tm": c - 2}),
        (a_ok, {"tm": c + 2}),
        (relay_ok, {"tm": c - 1}),
        (relayed, {"tm": c + 1}),
        ((far >= 0) & (far < groups), {"tm": far}),
        (s >= 1, {"space": s - 1}),
        (s + 1 < spaces, {"space": s + 1}),
    ]
    barrier = pltpu.get_barrier_semaphore()
    for valid, where in partners:
        def greet(where=where):
            pl.semaphore_signal(barrier, inc=1, device_id=where, device_id_type=MESH)
        if valid is None:
            greet()
        else:
            pl.when(valid)(greet)
    count = 1
    for valid, _ in partners[1:]:
        count = count + valid.astype(jnp.int32)
    pl.semaphore_wait(barrier, count)

    def columns(j):
        return pl.ds(pl.multiple_of(j * span, span), span)

    def remote(src, dst, send, recv, where):
        return pltpu.make_async_remote_copy(
            src_ref=src, dst_ref=dst, send_sem=send, recv_sem=recv,
            device_id=where, device_id_type=MESH,
        )

    def slot_rows(slot):
        return pl.ds(pl.multiple_of(slot * TILE, TILE), TILE)

    side_ok = (s >= 1, s + 1 < spaces)
    side_id = ({"space": s - 1}, {"space": s + 1})

    def q_copy(side, j):
        other = 1 - side
        return remote(
            q_hbm.at[:, columns(j)],
            qbuf.at[pl.ds(other * 2 * TILE, TILE), columns(j)],
            q_send.at[side, j], q_recv.at[other, j], side_id[side],
        )

    def q_wait(side, j):
        remote(
            q_hbm.at[:, columns(j)],
            qbuf.at[pl.ds(side * 2 * TILE, TILE), columns(j)],
            q_send.at[side, j], q_recv.at[side, j], side_id[side],
        ).wait_recv()

    to_b = c + 1 + 2 * parity
    slot_b = 1 + 2 * parity
    slot_f = 3 - 2 * parity
    b_ok = to_b < groups
    f_ok = c >= 2

    def a_copy(t, j):
        return remote(
            cleans[t].at[:, columns(j)], kv.at[t, pl.ds(2 * TILE, TILE), columns(j)],
            a_send.at[t, j], kv_recv.at[1, t, j], {"tm": c + 2},
        )

    def b_copy(t, j):
        return remote(
            cleans[t].at[:, columns(j)], kv.at[t, slot_rows(slot_b), columns(j)],
            b_send.at[t, j], kv_recv.at[slot_b - 1, t, j], {"tm": to_b},
        )

    def f_copy(t, j):
        return remote(
            kv.at[t, pl.ds(2 * TILE, TILE), columns(j)], kv.at[t, slot_rows(slot_f), columns(j)],
            f_send.at[t, j], kv_recv.at[slot_f - 1, t, j], {"tm": sibling},
        )

    def r_copy(t, j):
        return remote(
            kv.at[t, pl.ds(3 * TILE, TILE), columns(j)], kv.at[t, pl.ds(2 * TILE, TILE), columns(j)],
            r_send.at[t, j], kv_recv.at[1, t, j], {"tm": c - 1},
        )

    def kv_wait(slot, t, j):
        remote(
            cleans[t].at[:, columns(j)], kv.at[t, pl.ds(slot * TILE, TILE), columns(j)],
            a_send.at[t, j], kv_recv.at[slot - 1, t, j], {"tm": sibling},
        ).wait_recv()

    def o_rows(j):
        return pl.ds(pl.multiple_of(j * span, span), span)

    def o_copies(side, j):
        other = 1 - side
        return (
            remote(
                send_o.at[side, o_rows(j)], got_o.at[other, o_rows(j)],
                o_send.at[side, j], o_recv.at[other, j], side_id[side],
            ),
            remote(
                send_st.at[side, j], got_st.at[other, j],
                st_send.at[side, j], st_recv.at[other, j], side_id[side],
            ),
        )

    def o_wait(side, j):
        remote(
            send_o.at[side, o_rows(j)], got_o.at[side, o_rows(j)],
            o_send.at[side, j], o_recv.at[side, j], side_id[side],
        ).wait_recv()
        remote(
            send_st.at[side, j], got_st.at[side, j],
            st_send.at[side, j], st_recv.at[side, j], side_id[side],
        ).wait_recv()

    def start_sends(j):
        @pl.when(a_ok)
        def _():
            for t in range(2):
                a_copy(t, j).start()

        for side in range(2):
            @pl.when(side_ok[side])
            def _():
                q_copy(side, j).start()

    def wait_sends(j):
        @pl.when(a_ok)
        def _():
            for t in range(2):
                a_copy(t, j).wait_send()

        for side in range(2):
            @pl.when(side_ok[side])
            def _():
                q_copy(side, j).wait_send()

    for j in range(CHUNKS):
        @pl.when(b_ok)
        def _():
            for t in range(2):
                b_copy(t, j).start()

        if j < AHEAD:
            start_sends(j)

    for slot in range(1, SLOTS):
        @pl.when(c < slot)
        def _():
            kv[:, slot * TILE:(slot + 1) * TILE, :] = jnp.zeros((2, TILE, width), kv.dtype)
    for side in range(2):
        @pl.when(jnp.logical_not(side_ok[side]))
        def _():
            qbuf[side * 2 * TILE:side * 2 * TILE + TILE, :] = jnp.zeros((TILE, width), qbuf.dtype)
            got_o[side] = jnp.zeros(got_o.shape[1:], got_o.dtype)
            got_st[side] = jnp.zeros(got_st.shape[1:], got_st.dtype)

    for copy in locals_[:3]:
        copy.wait()

    bias = [None] + [jnp.where(c >= d, 0.0, LOW).astype(jnp.float32) for d in range(1, SLOTS)]

    def relay(j):
        @pl.when(relay_ok)
        def _():
            for t in range(2):
                kv_wait(3, t, j)
                r_copy(t, j).start()

    relay(0)

    def attend(j, carry):
        @pl.when(j + AHEAD < CHUNKS)
        def _():
            wait_sends(j)
            start_sends(j + AHEAD)

        @pl.when(f_ok)
        def _():
            for t in range(2):
                kv_wait(2, t, j)
                f_copy(t, j).start()

        @pl.when(j + 1 < CHUNKS)
        def _():
            relay(j + 1)

        for side in range(2):
            @pl.when(side_ok[side])
            def _():
                q_wait(side, j)

        for slot, awaited in ((1, c >= 1), (3, (c >= 3) & jnp.logical_not(relay_ok))):
            @pl.when(awaited)
            def _():
                for t in range(2):
                    kv_wait(slot, t, j)

        peaks, sums = [], []
        for h in range(heads):
            at = pl.multiple_of(j * span + h * HEAD, HEAD)
            q = qbuf[:, pl.ds(at, HEAD)]
            scores = []
            peak = None
            for d in range(SLOTS):
                k = kv[0, d * TILE:(d + 1) * TILE, pl.ds(at, HEAD)]
                part = lax.dot_general(
                    k, q, (((1,), (1,)), ((), ())), preferred_element_type=jnp.float32
                )
                top = jnp.max(part, axis=0, keepdims=True) * RATE
                if d > 0:
                    top = top + bias[d]
                peak = top if peak is None else jnp.maximum(peak, top)
                scores.append(part)
            total = None
            weights = []
            for d in range(SLOTS):
                shift = -peak if d == 0 else bias[d] - peak
                weight = jnp.exp2(scores[d] * RATE + shift)
                part = jnp.sum(weight, axis=0, keepdims=True)
                total = part if total is None else total + part
                weights.append(weight.astype(jnp.bfloat16))
            v = kv[1, :, pl.ds(at, HEAD)]
            numer = jnp.dot(
                v.T, jnp.concatenate(weights, axis=0), preferred_element_type=jnp.float32
            )
            rows = pl.ds(at, HEAD)
            own_o[rows, :] = numer[:, TILE:2 * TILE]
            send_o[0, rows, :] = numer[:, :TILE].astype(jnp.bfloat16)
            send_o[1, rows, :] = numer[:, 2 * TILE:].astype(jnp.bfloat16)
            peaks.append(peak)
            sums.append(total)
        filler = [jnp.zeros((8 - 2 * heads, 3 * TILE), jnp.float32)]
        stats = jnp.concatenate(peaks + sums + filler, axis=0)
        own_st[j] = stats[:, TILE:2 * TILE]
        send_st[0, j] = stats[:, :TILE]
        send_st[1, j] = stats[:, 2 * TILE:]
        for side in range(2):
            @pl.when(side_ok[side])
            def _():
                for copy in o_copies(side, j):
                    copy.start()
        return carry

    lax.fori_loop(0, CHUNKS, attend, 0)

    locals_[3].wait()
    allowed = (
        side_ok[0] & (mask_ref[0] == 1),
        side_ok[1] & (mask_ref[2] == 1),
    )
    noise = noise_ref[0]
    gate = gate_ref[0:1, :]
    for level in range(1, gate_ref.shape[0]):
        gate = jnp.where(noise == level, gate_ref[level:level + 1, :], gate)

    projected = jnp.zeros((TILE, wbuf.shape[1]), jnp.float32)
    for j in range(CHUNKS):
        for side in range(2):
            @pl.when(side_ok[side])
            def _():
                o_wait(side, j)
        merged = []
        for h in range(heads):
            rows = slice(j * span + h * HEAD, j * span + (h + 1) * HEAD)
            mine = own_st[j, h:h + 1, :]
            tops = [
                jnp.where(allowed[side], got_st[side, j, h:h + 1, :], LOW) for side in range(2)
            ]
            peak = jnp.maximum(mine, jnp.maximum(tops[0], tops[1]))
            factor = jnp.exp2(mine - peak)
            total = factor * own_st[j, heads + h:heads + h + 1, :]
            numer = factor * own_o[rows, :]
            for side in range(2):
                factor = jnp.exp2(tops[side] - peak)
                total = total + factor * got_st[side, j, heads + h:heads + h + 1, :]
                numer = numer + factor * got_o[side, rows, :].astype(jnp.float32)
            merged.append((numer / total).T.astype(jnp.bfloat16))
        projected = projected + jnp.dot(
            jnp.concatenate(merged, axis=1), wbuf[j * span:(j + 1) * span, :],
            preferred_element_type=jnp.float32,
        )
    out_ref[...] = (gate * projected).astype(out_ref.dtype)

    for j in range(CHUNKS - AHEAD, CHUNKS):
        wait_sends(j)

    def drain(j, carry):
        @pl.when(relay_ok)
        def _():
            for t in range(2):
                r_copy(t, j).wait_send()

        @pl.when(b_ok)
        def _():
            for t in range(2):
                b_copy(t, j).wait_send()

        @pl.when(f_ok)
        def _():
            for t in range(2):
                f_copy(t, j).wait_send()

        for side in range(2):
            @pl.when(side_ok[side])
            def _():
                for copy in o_copies(side, j):
                    copy.wait_send()
        return carry

    lax.fori_loop(0, CHUNKS, drain, 0)


def on_device(
    groups, spaces,
    query, key_new, value_new, key_clean, value_clean, out_weight, step_gate, noise_step, tile_mask,
):
    width = query.shape[2]
    anywhere = pl.BlockSpec(memory_space=pl.ANY)
    vmem = pl.BlockSpec(memory_space=pltpu.VMEM)
    smem = pl.BlockSpec(memory_space=pltpu.SMEM)
    dma = pltpu.SemaphoreType.DMA
    out = pl.pallas_call(
        functools.partial(kernel, groups, spaces),
        out_shape=pltpu.VMEM((TILE, out_weight.shape[1]), jnp.bfloat16),
        in_specs=[anywhere] * 6 + [vmem, smem, smem],
        out_specs=vmem,
        scratch_shapes=[
            pltpu.VMEM((3 * TILE, width), jnp.bfloat16),
            pltpu.VMEM((2, SLOTS * TILE, width), jnp.bfloat16),
            pltpu.VMEM(out_weight.shape, jnp.bfloat16),
            pltpu.VMEM((width, TILE), jnp.float32),
            pltpu.VMEM((CHUNKS, 8, TILE), jnp.float32),
            pltpu.VMEM((2, width, TILE), jnp.bfloat16),
            pltpu.VMEM((2, CHUNKS, 8, TILE), jnp.float32),
            pltpu.VMEM((2, width, TILE), jnp.bfloat16),
            pltpu.VMEM((2, CHUNKS, 8, TILE), jnp.float32),
            dma((4,)),
            dma((2, CHUNKS)), dma((2, CHUNKS)),
            dma((PAST, 2, CHUNKS)),
            dma((2, CHUNKS)), dma((2, CHUNKS)), dma((2, CHUNKS)), dma((2, CHUNKS)),
            dma((2, CHUNKS)), dma((2, CHUNKS)),
            dma((2, CHUNKS)), dma((2, CHUNKS)),
        ],
        compiler_params=pltpu.CompilerParams(
            collective_id=0, has_side_effects=True, vmem_limit_bytes=56 * 2**20
        ),
        name="tile_attention",
    )(
        query[0], key_new[0], value_new[0], key_clean[0], value_clean[0], out_weight,
        step_gate, noise_step, tile_mask.reshape(-1),
    )
    return out[None]


def solution(mesh):
    split = P("tm", "space", None)
    placed = (split, split, split, split, split, P(), P(), P("tm"), split)
    return jax.shard_map(
        functools.partial(on_device, mesh.shape["tm"], mesh.shape["space"]),
        mesh=mesh, in_specs=placed, out_specs=split, check_vma=False,
    )
```

```python
import functools
import math

import jax
import jax.numpy as jnp
from jax import lax
from jax.experimental import pallas as pl
from jax.experimental.pallas import tpu as pltpu
from jax.sharding import PartitionSpec as P

HEAD = 128
TILE = 128
PAST = 3
SLOTS = PAST + 1
AHEAD = 3
PAIR = 2
LOW = -1e30
RATE = math.log2(math.e) / math.sqrt(HEAD)
MESH = pl.DeviceIdType.MESH


def kernel(
    groups, spaces,
    q_hbm, kn_hbm, vn_hbm, kc_hbm, vc_hbm, w_hbm, gate_hbm, noise_hbm, mask_hbm,
    out_ref,
    gate_ref, noise_ref, mask_ref, projected, qbuf, kv, wbuf, own_o, own_st, send_o, send_st, got_o, got_st,
    local_sem, q_send, q_recv, kv_recv, a_send, b_send, f_send, r_send, o_send, o_recv, st_send, st_recv,
):
    c = lax.axis_index("tm")
    s = lax.axis_index("space")
    parity = lax.rem(c, 2)
    width = q_hbm.shape[1]
    pairs = width // HEAD // PAIR - 1
    chunks = pairs + 2
    span = PAIR * HEAD
    cleans = (kc_hbm, vc_hbm)

    sibling = c + 1 - 2 * parity
    far = c - 3 + 6 * parity
    corner = lax.rem(c, 4)
    a_ok = (c + 2 < groups) & jnp.logical_not((corner == 3) & (c + 3 < groups))
    relay_ok = (corner == 2) & (c >= 3)
    relayed = (corner == 1) & (c >= 2) & (c + 1 < groups)
    partners = [
        (None, {"tm": sibling}),
        ((c >= 2) & jnp.logical_not(relayed), {"tm": c - 2}),
        (a_ok, {"tm": c + 2}),
        (relay_ok, {"tm": c - 1}),
        (relayed, {"tm": c + 1}),
        ((far >= 0) & (far < groups), {"tm": far}),
        (s >= 1, {"space": s - 1}),
        (s + 1 < spaces, {"space": s + 1}),
    ]
    barrier = pltpu.get_barrier_semaphore()
    for valid, where in partners:
        def greet(where=where):
            pl.semaphore_signal(barrier, inc=1, device_id=where, device_id_type=MESH)
        if valid is None:
            greet()
        else:
            pl.when(valid)(greet)
    locals_ = [
        pltpu.make_async_copy(src, dst, local_sem.at[i])
        for i, (src, dst) in enumerate((
            (q_hbm, qbuf.at[pl.ds(TILE, TILE)]),
            (kn_hbm, kv.at[0, pl.ds(0, TILE)]),
            (vn_hbm, kv.at[1, pl.ds(0, TILE)]),
            (w_hbm, wbuf),
            (gate_hbm, gate_ref),
            (noise_hbm, noise_ref),
            (mask_hbm, mask_ref),
        ))
    ]
    for copy in locals_:
        copy.start()

    count = 1
    for valid, _ in partners[1:]:
        count = count + valid.astype(jnp.int32)
    pl.semaphore_wait(barrier, count)

    def heads_of(j):
        return PAIR if not isinstance(j, int) or j < pairs else 1

    def start_of(j):
        if isinstance(j, int):
            return j * span if j < pairs else pairs * span + (j - pairs) * HEAD
        return pl.multiple_of(j * span, span)

    def columns(j):
        return pl.ds(start_of(j), heads_of(j) * HEAD)

    def remote(src, dst, send, recv, where):
        return pltpu.make_async_remote_copy(
            src_ref=src, dst_ref=dst, send_sem=send, recv_sem=recv,
            device_id=where, device_id_type=MESH,
        )

    def slot_rows(slot):
        return pl.ds(pl.multiple_of(slot * TILE, TILE), TILE)

    side_ok = (s >= 1, s + 1 < spaces)
    side_id = ({"space": s - 1}, {"space": s + 1})

    def q_copy(side, j):
        other = 1 - side
        return remote(
            q_hbm.at[:, columns(j)],
            qbuf.at[pl.ds(other * 2 * TILE, TILE), columns(j)],
            q_send.at[side, j], q_recv.at[other, j], side_id[side],
        )

    def q_wait(side, j):
        remote(
            q_hbm.at[:, columns(j)],
            qbuf.at[pl.ds(side * 2 * TILE, TILE), columns(j)],
            q_send.at[side, j], q_recv.at[side, j], side_id[side],
        ).wait_recv()

    to_b = c + 1 + 2 * parity
    slot_b = 1 + 2 * parity
    slot_f = 3 - 2 * parity
    b_ok = to_b < groups
    f_ok = c >= 2

    def a_copy(t, j):
        return remote(
            cleans[t].at[:, columns(j)], kv.at[t, pl.ds(2 * TILE, TILE), columns(j)],
            a_send.at[t, j], kv_recv.at[1, t, j], {"tm": c + 2},
        )

    def b_copy(t, j):
        return remote(
            cleans[t].at[:, columns(j)], kv.at[t, slot_rows(slot_b), columns(j)],
            b_send.at[t, j], kv_recv.at[slot_b - 1, t, j], {"tm": to_b},
        )

    def f_copy(t, j):
        return remote(
            kv.at[t, pl.ds(2 * TILE, TILE), columns(j)], kv.at[t, slot_rows(slot_f), columns(j)],
            f_send.at[t, j], kv_recv.at[slot_f - 1, t, j], {"tm": sibling},
        )

    def r_copy(t, j):
        return remote(
            kv.at[t, pl.ds(3 * TILE, TILE), columns(j)], kv.at[t, pl.ds(2 * TILE, TILE), columns(j)],
            r_send.at[t, j], kv_recv.at[1, t, j], {"tm": c - 1},
        )

    def kv_wait(slot, t, j):
        remote(
            cleans[t].at[:, columns(j)], kv.at[t, pl.ds(slot * TILE, TILE), columns(j)],
            a_send.at[t, j], kv_recv.at[slot - 1, t, j], {"tm": sibling},
        ).wait_recv()

    def o_copies(side, j):
        other = 1 - side
        return (
            remote(
                send_o.at[side, columns(j)], got_o.at[other, columns(j)],
                o_send.at[side, j], o_recv.at[other, j], side_id[side],
            ),
            remote(
                send_st.at[side, j], got_st.at[other, j],
                st_send.at[side, j], st_recv.at[other, j], side_id[side],
            ),
        )

    def o_wait(side, j):
        remote(
            send_o.at[side, columns(j)], got_o.at[side, columns(j)],
            o_send.at[side, j], o_recv.at[side, j], side_id[side],
        ).wait_recv()
        remote(
            send_st.at[side, j], got_st.at[side, j],
            st_send.at[side, j], st_recv.at[side, j], side_id[side],
        ).wait_recv()

    def start_sends(j):
        @pl.when(a_ok)
        def _():
            for t in range(2):
                a_copy(t, j).start()

        for side in range(2):
            @pl.when(side_ok[side])
            def _():
                q_copy(side, j).start()

    def wait_sends(j):
        @pl.when(a_ok)
        def _():
            for t in range(2):
                a_copy(t, j).wait_send()

        for side in range(2):
            @pl.when(side_ok[side])
            def _():
                q_copy(side, j).wait_send()

    for j in range(chunks):
        if j < AHEAD:
            start_sends(j)

        @pl.when(b_ok)
        def _():
            for t in range(2):
                b_copy(t, j).start()

    for slot in range(1, SLOTS):
        @pl.when(c < slot)
        def _():
            kv[:, slot * TILE:(slot + 1) * TILE, :] = jnp.zeros((2, TILE, width), kv.dtype)
    for side in range(2):
        @pl.when(jnp.logical_not(side_ok[side]))
        def _():
            qbuf[side * 2 * TILE:side * 2 * TILE + TILE, :] = jnp.zeros((TILE, width), qbuf.dtype)
            got_o[side] = jnp.zeros(got_o.shape[1:], got_o.dtype)
            got_st[side] = jnp.zeros(got_st.shape[1:], got_st.dtype)

    for copy in locals_[:3]:
        copy.wait()

    bias = [None] + [jnp.where(c >= d, 0.0, LOW).astype(jnp.float32) for d in range(1, SLOTS)]

    def relay(j):
        @pl.when(relay_ok)
        def _():
            for t in range(2):
                kv_wait(3, t, j)
                r_copy(t, j).start()

    relay(0)

    def attend(j):
        if not isinstance(j, int):
            wait_sends(j)

            @pl.when(j + AHEAD < pairs)
            def _():
                start_sends(j + AHEAD)

            @pl.when(j + AHEAD == pairs)
            def _():
                start_sends(pairs)
                start_sends(pairs + 1)

        @pl.when(f_ok)
        def _():
            for t in range(2):
                kv_wait(2, t, j)
                f_copy(t, j).start()

        if isinstance(j, int):
            if j + 1 < chunks:
                relay(j + 1)
        else:
            @pl.when(j + 1 < pairs)
            def _():
                relay(j + 1)

            @pl.when(j + 1 == pairs)
            def _():
                relay(pairs)

        for side in range(2):
            @pl.when(side_ok[side])
            def _():
                q_wait(side, j)

        for slot, awaited in ((1, c >= 1), (3, (c >= 3) & jnp.logical_not(relay_ok))):
            @pl.when(awaited)
            def _():
                for t in range(2):
                    kv_wait(slot, t, j)

        peaks, sums = [], []
        heads = heads_of(j)
        for h in range(heads):
            at = start_of(j) + h * HEAD
            if not isinstance(j, int):
                at = pl.multiple_of(at, HEAD)
            q = qbuf[:, pl.ds(at, HEAD)]
            scores = []
            peak = None
            for d in range(SLOTS):
                k = kv[0, d * TILE:(d + 1) * TILE, pl.ds(at, HEAD)]
                part = lax.dot_general(
                    k, q, (((1,), (1,)), ((), ())), preferred_element_type=jnp.float32
                )
                top = jnp.max(part, axis=0, keepdims=True) * RATE
                if d > 0:
                    top = top + bias[d]
                peak = top if peak is None else jnp.maximum(peak, top)
                scores.append(part)
            total = None
            weights = []
            for d in range(SLOTS):
                shift = -peak if d == 0 else bias[d] - peak
                weight = jnp.exp2(scores[d] * RATE + shift)
                part = jnp.sum(weight, axis=0, keepdims=True)
                total = part if total is None else total + part
                weights.append(weight.astype(jnp.bfloat16))
            v = kv[1, :, pl.ds(at, HEAD)]
            numer = jnp.dot(
                v.T, jnp.concatenate(weights, axis=0), preferred_element_type=jnp.float32
            )
            rows = pl.ds(at, HEAD)
            own_o[rows, :] = numer[:, TILE:2 * TILE]
            send_o[0, rows, :] = numer[:, :TILE].astype(jnp.bfloat16)
            send_o[1, rows, :] = numer[:, 2 * TILE:].astype(jnp.bfloat16)
            peaks.append(peak)
            sums.append(total)
        filler = [jnp.zeros((8 - 2 * heads, 3 * TILE), jnp.float32)]
        stats = jnp.concatenate(peaks + sums + filler, axis=0)
        own_st[j] = stats[:, TILE:2 * TILE]
        send_st[0, j] = stats[:, :TILE]
        send_st[1, j] = stats[:, 2 * TILE:]
        for side in range(2):
            @pl.when(side_ok[side])
            def _():
                for copy in o_copies(side, j):
                    copy.start()

    for copy in locals_[3:]:
        copy.wait()
    allowed = (
        side_ok[0] & (mask_ref[0] == 1),
        side_ok[1] & (mask_ref[2] == 1),
    )
    projected[...] = jnp.zeros(projected.shape, projected.dtype)

    def merge(j):
        for side in range(2):
            @pl.when(side_ok[side])
            def _():
                o_wait(side, j)
        merged = []
        heads = heads_of(j)
        for h in range(heads):
            at = start_of(j) + h * HEAD
            if not isinstance(j, int):
                at = pl.multiple_of(at, HEAD)
            rows = pl.ds(at, HEAD)
            mine = own_st[j, h:h + 1, :]
            tops = [
                jnp.where(allowed[side], got_st[side, j, h:h + 1, :], LOW) for side in range(2)
            ]
            peak = jnp.maximum(mine, jnp.maximum(tops[0], tops[1]))
            factor = jnp.exp2(mine - peak)
            total = factor * own_st[j, heads + h:heads + h + 1, :]
            numer = factor * own_o[rows, :]
            for side in range(2):
                factor = jnp.exp2(tops[side] - peak)
                total = total + factor * got_st[side, j, heads + h:heads + h + 1, :]
                numer = numer + factor * got_o[side, rows, :].astype(jnp.float32)
            merged.append((numer / total).T.astype(jnp.bfloat16))
        left = merged[0] if heads == 1 else jnp.concatenate(merged, axis=1)
        return jnp.dot(left, wbuf[columns(j), :], preferred_element_type=jnp.float32)

    def step(j, carry):
        attend(j)

        @pl.when(j >= 2)
        def _():
            projected[...] += merge(j - 2)
        return carry

    lax.fori_loop(0, pairs, step, 0)
    attend(pairs)
    projected[...] += merge(pairs - 2)
    attend(pairs + 1)
    projected[...] += merge(pairs - 1)
    noise = noise_ref[0]
    gate = gate_ref[0:1, :]
    for level in range(1, gate_ref.shape[0]):
        gate = jnp.where(noise == level, gate_ref[level:level + 1, :], gate)
    projected[...] += merge(pairs)
    out_ref[...] = (gate * (projected[...] + merge(pairs + 1))).astype(out_ref.dtype)

    wait_sends(pairs)
    wait_sends(pairs + 1)

    def drain(j):
        @pl.when(relay_ok)
        def _():
            for t in range(2):
                r_copy(t, j).wait_send()

        @pl.when(b_ok)
        def _():
            for t in range(2):
                b_copy(t, j).wait_send()

        @pl.when(f_ok)
        def _():
            for t in range(2):
                f_copy(t, j).wait_send()

        for side in range(2):
            @pl.when(side_ok[side])
            def _():
                for copy in o_copies(side, j):
                    copy.wait_send()

    def drain_step(j, carry):
        drain(j)
        return carry

    lax.fori_loop(0, pairs, drain_step, 0)
    drain(pairs)
    drain(pairs + 1)


def on_device(
    groups, spaces,
    query, key_new, value_new, key_clean, value_clean, out_weight, step_gate, noise_step, tile_mask,
):
    width = query.shape[2]
    anywhere = pl.BlockSpec(memory_space=pl.ANY)
    vmem = pl.BlockSpec(memory_space=pltpu.VMEM)
    chunks = width // HEAD // PAIR + 1
    dma = pltpu.SemaphoreType.DMA
    out = pl.pallas_call(
        functools.partial(kernel, groups, spaces),
        out_shape=pltpu.VMEM((TILE, out_weight.shape[1]), jnp.bfloat16),
        in_specs=[anywhere] * 9,
        out_specs=vmem,
        scratch_shapes=[
            pltpu.VMEM(step_gate.shape, jnp.float32),
            pltpu.SMEM(noise_step.shape, jnp.int32),
            pltpu.SMEM((tile_mask.size,), jnp.int32),
            pltpu.VMEM((TILE, out_weight.shape[1]), jnp.float32),
            pltpu.VMEM((3 * TILE, width), jnp.bfloat16),
            pltpu.VMEM((2, SLOTS * TILE, width), jnp.bfloat16),
            pltpu.VMEM(out_weight.shape, jnp.bfloat16),
            pltpu.VMEM((width, TILE), jnp.float32),
            pltpu.VMEM((chunks, 8, TILE), jnp.float32),
            pltpu.VMEM((2, width, TILE), jnp.bfloat16),
            pltpu.VMEM((2, chunks, 8, TILE), jnp.float32),
            pltpu.VMEM((2, width, TILE), jnp.bfloat16),
            pltpu.VMEM((2, chunks, 8, TILE), jnp.float32),
            dma((7,)),
            dma((2, chunks)), dma((2, chunks)),
            dma((PAST, 2, chunks)),
            dma((2, chunks)), dma((2, chunks)), dma((2, chunks)), dma((2, chunks)),
            dma((2, chunks)), dma((2, chunks)),
            dma((2, chunks)), dma((2, chunks)),
        ],
        compiler_params=pltpu.CompilerParams(
            collective_id=0, has_side_effects=True, vmem_limit_bytes=56 * 2**20
        ),
        name="tile_attention",
    )(
        query[0], key_new[0], value_new[0], key_clean[0], value_clean[0], out_weight,
        step_gate, noise_step, tile_mask.reshape(-1),
    )
    return out[None]


def solution(mesh):
    split = P("tm", "space", None)
    placed = (split, split, split, split, split, P(), P(), P("tm"), split)
    return jax.shard_map(
        functools.partial(on_device, mesh.shape["tm"], mesh.shape["space"]),
        mesh=mesh, in_specs=placed, out_specs=split, check_vma=False,
    )
```

```python
import functools
import math

import jax
import jax.numpy as jnp
from jax import lax
from jax.experimental import pallas as pl
from jax.experimental.pallas import tpu as pltpu
from jax.sharding import PartitionSpec as P

HEAD = 128
TILE = 128
PAST = 3
SLOTS = PAST + 1
PAIR = 2
LOW = -1e30
RATE = math.log2(math.e) / math.sqrt(HEAD)
MESH = pl.DeviceIdType.MESH


def kernel(
    groups, spaces,
    q_hbm, kn_hbm, vn_hbm, kc_hbm, vc_hbm, w_hbm, gate_hbm, noise_hbm, mask_hbm,
    out_ref,
    gate_ref, noise_ref, mask_ref, projected, qbuf, kv, stage, wbuf, own_o, own_st, send_o, send_st, got_o, got_st,
    local_sem, q_send, q_recv, kv_recv, a_send, b_send, f_send, r_send, s_send, s_recv, o_send, o_recv, st_send, st_recv,
):
    c = lax.axis_index("tm")
    s = lax.axis_index("space")
    parity = lax.rem(c, 2)
    width = q_hbm.shape[1]
    pairs = width // HEAD // PAIR - 1
    chunks = pairs + 2
    span = PAIR * HEAD
    cleans = (kc_hbm, vc_hbm)

    sibling = c + 1 - 2 * parity
    far = c - 3 + 6 * parity
    corner = lax.rem(c, 4)
    a_ok = (c + 2 < groups) & jnp.logical_not((corner == 3) & (c + 3 < groups))
    relay_ok = (corner == 2) & (c >= 3)
    relayed = (corner == 1) & (c >= 2) & (c + 1 < groups)
    around = (corner == 2) & (c + 5 < groups)
    stager = (corner == 3) & (c >= 7)
    staged = (corner == 0) & (c >= 4) & (c + 3 < groups)
    partners = [
        (None, {"tm": sibling}),
        ((c >= 2) & jnp.logical_not(relayed), {"tm": c - 2}),
        (a_ok, {"tm": c + 2}),
        (relay_ok, {"tm": c - 1}),
        (relayed, {"tm": c + 1}),
        (around, {"tm": c + 5}),
        (stager, {"tm": c - 5}),
        (stager, {"tm": c - 3}),
        (staged, {"tm": c + 3}),
        ((far >= 0) & (far < groups), {"tm": far}),
        (s >= 1, {"space": s - 1}),
        (s + 1 < spaces, {"space": s + 1}),
    ]
    barrier = pltpu.get_barrier_semaphore()
    for valid, where in partners:
        def greet(where=where):
            pl.semaphore_signal(barrier, inc=1, device_id=where, device_id_type=MESH)
        if valid is None:
            greet()
        else:
            pl.when(valid)(greet)
    locals_ = [
        pltpu.make_async_copy(src, dst, local_sem.at[i])
        for i, (src, dst) in enumerate((
            (q_hbm, qbuf.at[pl.ds(TILE, TILE)]),
            (kn_hbm, kv.at[0, pl.ds(0, TILE)]),
            (vn_hbm, kv.at[1, pl.ds(0, TILE)]),
            (w_hbm, wbuf),
            (gate_hbm, gate_ref),
            (noise_hbm, noise_ref),
            (mask_hbm, mask_ref),
        ))
    ]
    for copy in locals_:
        copy.start()

    count = 1
    for valid, _ in partners[1:]:
        count = count + valid.astype(jnp.int32)
    pl.semaphore_wait(barrier, count)

    def heads_of(j):
        return PAIR if not isinstance(j, int) or j < pairs else 1

    def start_of(j):
        if isinstance(j, int):
            return j * span if j < pairs else pairs * span + (j - pairs) * HEAD
        return pl.multiple_of(j * span, span)

    def columns(j):
        return pl.ds(start_of(j), heads_of(j) * HEAD)

    def remote(src, dst, send, recv, where):
        return pltpu.make_async_remote_copy(
            src_ref=src, dst_ref=dst, send_sem=send, recv_sem=recv,
            device_id=where, device_id_type=MESH,
        )

    def slot_rows(slot):
        return pl.ds(pl.multiple_of(slot * TILE, TILE), TILE)

    side_ok = (s >= 1, s + 1 < spaces)
    side_id = ({"space": s - 1}, {"space": s + 1})

    def q_copy(side, j):
        other = 1 - side
        return remote(
            q_hbm.at[:, columns(j)],
            qbuf.at[pl.ds(other * 2 * TILE, TILE), columns(j)],
            q_send.at[side, j], q_recv.at[other, j], side_id[side],
        )

    def q_wait(side, j):
        remote(
            q_hbm.at[:, columns(j)],
            qbuf.at[pl.ds(side * 2 * TILE, TILE), columns(j)],
            q_send.at[side, j], q_recv.at[side, j], side_id[side],
        ).wait_recv()

    to_b = c + 1 + 2 * parity
    slot_b = 1 + 2 * parity
    slot_f = 3 - 2 * parity
    b_ok = to_b < groups
    f_ok = c >= 2

    def a_copy(t, j):
        return remote(
            cleans[t].at[:, columns(j)], kv.at[t, pl.ds(2 * TILE, TILE), columns(j)],
            a_send.at[t, j], kv_recv.at[1, t, j], {"tm": c + 2},
        )

    def b_copy(t, j):
        return remote(
            cleans[t].at[:, columns(j)], kv.at[t, slot_rows(slot_b), columns(j)],
            b_send.at[t, j], kv_recv.at[slot_b - 1, t, j], {"tm": to_b},
        )

    def f_copy(t, j):
        return remote(
            kv.at[t, pl.ds(2 * TILE, TILE), columns(j)], kv.at[t, slot_rows(slot_f), columns(j)],
            f_send.at[t, j], kv_recv.at[slot_f - 1, t, j], {"tm": sibling},
        )

    def r_copy(t, j):
        return remote(
            kv.at[t, pl.ds(3 * TILE, TILE), columns(j)], kv.at[t, pl.ds(2 * TILE, TILE), columns(j)],
            r_send.at[t, j], kv_recv.at[1, t, j], {"tm": c - 1},
        )

    def d_copy(j):
        return remote(
            vc_hbm.at[:, columns(j)], stage.at[:, columns(j)],
            a_send.at[1, j], s_recv.at[j], {"tm": c + 5},
        )

    def s_wait(j):
        remote(
            vc_hbm.at[:, columns(j)], stage.at[:, columns(j)],
            a_send.at[1, j], s_recv.at[j], {"tm": sibling},
        ).wait_recv()

    def s_copy(j):
        return remote(
            stage.at[:, columns(j)], kv.at[1, pl.ds(2 * TILE, TILE), columns(j)],
            s_send.at[j], kv_recv.at[1, 1, j], {"tm": c - 3},
        )

    def kv_wait(slot, t, j):
        remote(
            cleans[t].at[:, columns(j)], kv.at[t, pl.ds(slot * TILE, TILE), columns(j)],
            a_send.at[t, j], kv_recv.at[slot - 1, t, j], {"tm": sibling},
        ).wait_recv()

    def o_copies(side, j):
        other = 1 - side
        return (
            remote(
                send_o.at[side, columns(j)], got_o.at[other, columns(j)],
                o_send.at[side, j], o_recv.at[other, j], side_id[side],
            ),
            remote(
                send_st.at[side, j], got_st.at[other, j],
                st_send.at[side, j], st_recv.at[other, j], side_id[side],
            ),
        )

    def o_wait(side, j):
        remote(
            send_o.at[side, columns(j)], got_o.at[side, columns(j)],
            o_send.at[side, j], o_recv.at[side, j], side_id[side],
        ).wait_recv()
        remote(
            send_st.at[side, j], got_st.at[side, j],
            st_send.at[side, j], st_recv.at[side, j], side_id[side],
        ).wait_recv()

    def start_sends(j):
        @pl.when(a_ok)
        def _():
            a_copy(0, j).start()

        @pl.when(a_ok & jnp.logical_not(around))
        def _():
            a_copy(1, j).start()

        @pl.when(around)
        def _():
            d_copy(j).start()

        for side in range(2):
            @pl.when(side_ok[side])
            def _():
                q_copy(side, j).start()

    def wait_sends(j):
        @pl.when(a_ok)
        def _():
            for t in range(2):
                a_copy(t, j).wait_send()

        for side in range(2):
            @pl.when(side_ok[side])
            def _():
                q_copy(side, j).wait_send()

    for j in range(chunks):
        start_sends(j)

        @pl.when(b_ok)
        def _():
            for t in range(2):
                b_copy(t, j).start()

    for slot in range(1, SLOTS):
        @pl.when(c < slot)
        def _():
            kv[:, slot * TILE:(slot + 1) * TILE, :] = jnp.zeros((2, TILE, width), kv.dtype)
    for side in range(2):
        @pl.when(jnp.logical_not(side_ok[side]))
        def _():
            qbuf[side * 2 * TILE:side * 2 * TILE + TILE, :] = jnp.zeros((TILE, width), qbuf.dtype)
            got_o[side] = jnp.zeros(got_o.shape[1:], got_o.dtype)
            got_st[side] = jnp.zeros(got_st.shape[1:], got_st.dtype)

    for copy in locals_[:3]:
        copy.wait()

    bias = [None] + [jnp.where(c >= d, 0.0, LOW).astype(jnp.float32) for d in range(1, SLOTS)]

    def relay(j):
        @pl.when(relay_ok)
        def _():
            for t in range(2):
                kv_wait(3, t, j)
                r_copy(t, j).start()

        @pl.when(stager)
        def _():
            s_wait(j)
            s_copy(j).start()

    relay(0)

    def attend(j):
        @pl.when(f_ok)
        def _():
            for t in range(2):
                kv_wait(2, t, j)
                f_copy(t, j).start()

        if isinstance(j, int):
            if j + 1 < chunks:
                relay(j + 1)
        else:
            @pl.when(j + 1 < pairs)
            def _():
                relay(j + 1)

            @pl.when(j + 1 == pairs)
            def _():
                relay(pairs)

        for side in range(2):
            @pl.when(side_ok[side])
            def _():
                q_wait(side, j)

        for slot, awaited in ((1, c >= 1), (3, (c >= 3) & jnp.logical_not(relay_ok))):
            @pl.when(awaited)
            def _():
                for t in range(2):
                    kv_wait(slot, t, j)

        peaks, sums = [], []
        heads = heads_of(j)
        for h in range(heads):
            at = start_of(j) + h * HEAD
            if not isinstance(j, int):
                at = pl.multiple_of(at, HEAD)
            q = qbuf[:, pl.ds(at, HEAD)]
            scores = []
            peak = None
            for d in range(SLOTS):
                k = kv[0, d * TILE:(d + 1) * TILE, pl.ds(at, HEAD)]
                part = lax.dot_general(
                    k, q, (((1,), (1,)), ((), ())), preferred_element_type=jnp.float32
                )
                top = jnp.max(part, axis=0, keepdims=True) * RATE
                if d > 0:
                    top = top + bias[d]
                peak = top if peak is None else jnp.maximum(peak, top)
                scores.append(part)
            total = None
            weights = []
            for d in range(SLOTS):
                shift = -peak if d == 0 else bias[d] - peak
                weight = jnp.exp2(scores[d] * RATE + shift)
                part = jnp.sum(weight, axis=0, keepdims=True)
                total = part if total is None else total + part
                weights.append(weight.astype(jnp.bfloat16))
            v = kv[1, :, pl.ds(at, HEAD)]
            numer = jnp.dot(
                v.T, jnp.concatenate(weights, axis=0), preferred_element_type=jnp.float32
            )
            rows = pl.ds(at, HEAD)
            own_o[rows, :] = numer[:, TILE:2 * TILE]
            send_o[0, rows, :] = numer[:, :TILE].astype(jnp.bfloat16)
            send_o[1, rows, :] = numer[:, 2 * TILE:].astype(jnp.bfloat16)
            peaks.append(peak)
            sums.append(total)
        filler = [jnp.zeros((8 - 2 * heads, 3 * TILE), jnp.float32)]
        stats = jnp.concatenate(peaks + sums + filler, axis=0)
        own_st[j] = stats[:, TILE:2 * TILE]
        send_st[0, j] = stats[:, :TILE]
        send_st[1, j] = stats[:, 2 * TILE:]
        for side in range(2):
            @pl.when(side_ok[side])
            def _():
                for copy in o_copies(side, j):
                    copy.start()

    for copy in locals_[3:]:
        copy.wait()
    allowed = (
        side_ok[0] & (mask_ref[0] == 1),
        side_ok[1] & (mask_ref[2] == 1),
    )
    projected[...] = jnp.zeros(projected.shape, projected.dtype)

    def merge(j):
        for side in range(2):
            @pl.when(side_ok[side])
            def _():
                o_wait(side, j)
        merged = []
        heads = heads_of(j)
        for h in range(heads):
            at = start_of(j) + h * HEAD
            if not isinstance(j, int):
                at = pl.multiple_of(at, HEAD)
            rows = pl.ds(at, HEAD)
            mine = own_st[j, h:h + 1, :]
            tops = [
                jnp.where(allowed[side], got_st[side, j, h:h + 1, :], LOW) for side in range(2)
            ]
            peak = jnp.maximum(mine, jnp.maximum(tops[0], tops[1]))
            factor = jnp.exp2(mine - peak)
            total = factor * own_st[j, heads + h:heads + h + 1, :]
            numer = factor * own_o[rows, :]
            for side in range(2):
                factor = jnp.exp2(tops[side] - peak)
                total = total + factor * got_st[side, j, heads + h:heads + h + 1, :]
                numer = numer + factor * got_o[side, rows, :].astype(jnp.float32)
            merged.append((numer / total).T.astype(jnp.bfloat16))
        left = merged[0] if heads == 1 else jnp.concatenate(merged, axis=1)
        return jnp.dot(left, wbuf[columns(j), :], preferred_element_type=jnp.float32)

    def step(j, carry):
        attend(j)

        @pl.when(j >= 2)
        def _():
            projected[...] += merge(j - 2)
        return carry

    lax.fori_loop(0, pairs, step, 0)
    attend(pairs)
    projected[...] += merge(pairs - 2)
    attend(pairs + 1)
    projected[...] += merge(pairs - 1)
    noise = noise_ref[0]
    gate = gate_ref[0:1, :]
    for level in range(1, gate_ref.shape[0]):
        gate = jnp.where(noise == level, gate_ref[level:level + 1, :], gate)
    projected[...] += merge(pairs)
    out_ref[...] = (gate * (projected[...] + merge(pairs + 1))).astype(out_ref.dtype)

    def drain(j):
        wait_sends(j)

        @pl.when(stager)
        def _():
            s_copy(j).wait_send()

        @pl.when(relay_ok)
        def _():
            for t in range(2):
                r_copy(t, j).wait_send()

        @pl.when(b_ok)
        def _():
            for t in range(2):
                b_copy(t, j).wait_send()

        @pl.when(f_ok)
        def _():
            for t in range(2):
                f_copy(t, j).wait_send()

        for side in range(2):
            @pl.when(side_ok[side])
            def _():
                for copy in o_copies(side, j):
                    copy.wait_send()

    def drain_step(j, carry):
        drain(j)
        return carry

    lax.fori_loop(0, pairs, drain_step, 0)
    drain(pairs)
    drain(pairs + 1)


def on_device(
    groups, spaces,
    query, key_new, value_new, key_clean, value_clean, out_weight, step_gate, noise_step, tile_mask,
):
    width = query.shape[2]
    anywhere = pl.BlockSpec(memory_space=pl.ANY)
    vmem = pl.BlockSpec(memory_space=pltpu.VMEM)
    chunks = width // HEAD // PAIR + 1
    dma = pltpu.SemaphoreType.DMA
    out = pl.pallas_call(
        functools.partial(kernel, groups, spaces),
        out_shape=pltpu.VMEM((TILE, out_weight.shape[1]), jnp.bfloat16),
        in_specs=[anywhere] * 9,
        out_specs=vmem,
        scratch_shapes=[
            pltpu.VMEM(step_gate.shape, jnp.float32),
            pltpu.SMEM(noise_step.shape, jnp.int32),
            pltpu.SMEM((tile_mask.size,), jnp.int32),
            pltpu.VMEM((TILE, out_weight.shape[1]), jnp.float32),
            pltpu.VMEM((3 * TILE, width), jnp.bfloat16),
            pltpu.VMEM((2, SLOTS * TILE, width), jnp.bfloat16),
            pltpu.VMEM((TILE, width), jnp.bfloat16),
            pltpu.VMEM(out_weight.shape, jnp.bfloat16),
            pltpu.VMEM((width, TILE), jnp.float32),
            pltpu.VMEM((chunks, 8, TILE), jnp.float32),
            pltpu.VMEM((2, width, TILE), jnp.bfloat16),
            pltpu.VMEM((2, chunks, 8, TILE), jnp.float32),
            pltpu.VMEM((2, width, TILE), jnp.bfloat16),
            pltpu.VMEM((2, chunks, 8, TILE), jnp.float32),
            dma((7,)),
            dma((2, chunks)), dma((2, chunks)),
            dma((PAST, 2, chunks)),
            dma((2, chunks)), dma((2, chunks)), dma((2, chunks)), dma((2, chunks)),
            dma((chunks,)), dma((chunks,)),
            dma((2, chunks)), dma((2, chunks)),
            dma((2, chunks)), dma((2, chunks)),
        ],
        compiler_params=pltpu.CompilerParams(
            collective_id=0, has_side_effects=True, vmem_limit_bytes=56 * 2**20
        ),
        name="tile_attention",
    )(
        query[0], key_new[0], value_new[0], key_clean[0], value_clean[0], out_weight,
        step_gate, noise_step, tile_mask.reshape(-1),
    )
    return out[None]


def solution(mesh):
    split = P("tm", "space", None)
    placed = (split, split, split, split, split, P(), P(), P("tm"), split)
    return jax.shard_map(
        functools.partial(on_device, mesh.shape["tm"], mesh.shape["space"]),
        mesh=mesh, in_specs=placed, out_specs=split, check_vma=False,
    )
```

```python
import functools
import math

import jax
import jax.numpy as jnp
from jax import lax
from jax.experimental import pallas as pl
from jax.experimental.pallas import tpu as pltpu
from jax.sharding import PartitionSpec as P

HEAD = 128
TILE = 128
PAST = 3
SLOTS = PAST + 1
CHUNKS = 6
AHEAD = 3
LOW = -1e30
RATE = math.log2(math.e) / math.sqrt(HEAD)
MESH = pl.DeviceIdType.MESH


def kernel(
    groups, spaces,
    q_hbm, kn_hbm, vn_hbm, kc_hbm, vc_hbm, w_hbm, gate_ref, noise_ref, mask_ref,
    out_ref,
    qbuf, kv, wbuf, own_o, own_st, send_o, send_st, got_o, got_st,
    local_sem, q_send, q_recv, kv_recv, a_send, b_send, f_send, r_send, o_send, o_recv, st_send, st_recv,
):
    c = lax.axis_index("tm")
    s = lax.axis_index("space")
    parity = lax.rem(c, 2)
    width = q_hbm.shape[1]
    span = width // CHUNKS
    heads = span // HEAD
    cleans = (kc_hbm, vc_hbm)

    locals_ = [
        pltpu.make_async_copy(q_hbm, qbuf.at[pl.ds(TILE, TILE)], local_sem.at[0]),
        pltpu.make_async_copy(kn_hbm, kv.at[0, pl.ds(0, TILE)], local_sem.at[1]),
        pltpu.make_async_copy(vn_hbm, kv.at[1, pl.ds(0, TILE)], local_sem.at[2]),
        pltpu.make_async_copy(w_hbm, wbuf, local_sem.at[3]),
    ]
    for copy in locals_:
        copy.start()

    sibling = c + 1 - 2 * parity
    far = c - 3 + 6 * parity
    corner = lax.rem(c, 4)
    a_ok = (c + 2 < groups) & jnp.logical_not((corner == 3) & (c + 3 < groups))
    relay_ok = (corner == 2) & (c >= 3)
    relayed = (corner == 1) & (c >= 2) & (c + 1 < groups)
    partners = [
        (None, {"tm": sibling}),
        ((c >= 2) & jnp.logical_not(relayed), {"tm": c - 2}),
        (a_ok, {"tm": c + 2}),
        (relay_ok, {"tm": c - 1}),
        (relayed, {"tm": c + 1}),
        ((far >= 0) & (far < groups), {"tm": far}),
        (s >= 1, {"space": s - 1}),
        (s + 1 < spaces, {"space": s + 1}),
    ]
    barrier = pltpu.get_barrier_semaphore()
    for valid, where in partners:
        def greet(where=where):
            pl.semaphore_signal(barrier, inc=1, device_id=where, device_id_type=MESH)
        if valid is None:
            greet()
        else:
            pl.when(valid)(greet)
    count = 1
    for valid, _ in partners[1:]:
        count = count + valid.astype(jnp.int32)
    pl.semaphore_wait(barrier, count)

    def columns(j):
        return pl.ds(pl.multiple_of(j * span, span), span)

    def remote(src, dst, send, recv, where):
        return pltpu.make_async_remote_copy(
            src_ref=src, dst_ref=dst, send_sem=send, recv_sem=recv,
            device_id=where, device_id_type=MESH,
        )

    def slot_rows(slot):
        return pl.ds(pl.multiple_of(slot * TILE, TILE), TILE)

    side_ok = (s >= 1, s + 1 < spaces)
    side_id = ({"space": s - 1}, {"space": s + 1})

    def q_copy(side, j):
        other = 1 - side
        return remote(
            q_hbm.at[:, columns(j)],
            qbuf.at[pl.ds(other * 2 * TILE, TILE), columns(j)],
            q_send.at[side, j], q_recv.at[other, j], side_id[side],
        )

    def q_wait(side, j):
        remote(
            q_hbm.at[:, columns(j)],
            qbuf.at[pl.ds(side * 2 * TILE, TILE), columns(j)],
            q_send.at[side, j], q_recv.at[side, j], side_id[side],
        ).wait_recv()

    to_b = c + 1 + 2 * parity
    slot_b = 1 + 2 * parity
    slot_f = 3 - 2 * parity
    b_ok = to_b < groups
    f_ok = c >= 2

    def a_copy(t, j):
        return remote(
            cleans[t].at[:, columns(j)], kv.at[t, pl.ds(2 * TILE, TILE), columns(j)],
            a_send.at[t, j], kv_recv.at[1, t, j], {"tm": c + 2},
        )

    def b_copy(t, j):
        return remote(
            cleans[t].at[:, columns(j)], kv.at[t, slot_rows(slot_b), columns(j)],
            b_send.at[t, j], kv_recv.at[slot_b - 1, t, j], {"tm": to_b},
        )

    def f_copy(t, j):
        return remote(
            kv.at[t, pl.ds(2 * TILE, TILE), columns(j)], kv.at[t, slot_rows(slot_f), columns(j)],
            f_send.at[t, j], kv_recv.at[slot_f - 1, t, j], {"tm": sibling},
        )

    def r_copy(t, j):
        return remote(
            kv.at[t, pl.ds(3 * TILE, TILE), columns(j)], kv.at[t, pl.ds(2 * TILE, TILE), columns(j)],
            r_send.at[t, j], kv_recv.at[1, t, j], {"tm": c - 1},
        )

    def kv_wait(slot, t, j):
        remote(
            cleans[t].at[:, columns(j)], kv.at[t, pl.ds(slot * TILE, TILE), columns(j)],
            a_send.at[t, j], kv_recv.at[slot - 1, t, j], {"tm": sibling},
        ).wait_recv()

    def o_copies(side, j):
        other = 1 - side
        return (
            remote(
                send_o.at[side, :, columns(j)], got_o.at[other, :, columns(j)],
                o_send.at[side, j], o_recv.at[other, j], side_id[side],
            ),
            remote(
                send_st.at[side, j], got_st.at[other, j],
                st_send.at[side, j], st_recv.at[other, j], side_id[side],
            ),
        )

    def o_wait(side, j):
        remote(
            send_o.at[side, :, columns(j)], got_o.at[side, :, columns(j)],
            o_send.at[side, j], o_recv.at[side, j], side_id[side],
        ).wait_recv()
        remote(
            send_st.at[side, j], got_st.at[side, j],
            st_send.at[side, j], st_recv.at[side, j], side_id[side],
        ).wait_recv()

    def start_sends(j):
        @pl.when(a_ok)
        def _():
            for t in range(2):
                a_copy(t, j).start()

        for side in range(2):
            @pl.when(side_ok[side])
            def _():
                q_copy(side, j).start()

    def wait_sends(j):
        @pl.when(a_ok)
        def _():
            for t in range(2):
                a_copy(t, j).wait_send()

        for side in range(2):
            @pl.when(side_ok[side])
            def _():
                q_copy(side, j).wait_send()

    for j in range(CHUNKS):
        @pl.when(b_ok)
        def _():
            for t in range(2):
                b_copy(t, j).start()

        if j < AHEAD:
            start_sends(j)

    for slot in range(1, SLOTS):
        @pl.when(c < slot)
        def _():
            kv[:, slot * TILE:(slot + 1) * TILE, :] = jnp.zeros((2, TILE, width), kv.dtype)
    for side in range(2):
        @pl.when(jnp.logical_not(side_ok[side]))
        def _():
            qbuf[side * 2 * TILE:side * 2 * TILE + TILE, :] = jnp.zeros((TILE, width), qbuf.dtype)
            got_o[side] = jnp.zeros(got_o.shape[1:], got_o.dtype)
            got_st[side] = jnp.zeros(got_st.shape[1:], got_st.dtype)

    for copy in locals_[:3]:
        copy.wait()

    bias = [None] + [jnp.where(c >= d, 0.0, LOW).astype(jnp.float32) for d in range(1, SLOTS)]

    def relay(j):
        @pl.when(relay_ok)
        def _():
            for t in range(2):
                kv_wait(3, t, j)
                r_copy(t, j).start()

    relay(0)

    def attend(j, carry):
        @pl.when(j + AHEAD < CHUNKS)
        def _():
            wait_sends(j)
            start_sends(j + AHEAD)

        @pl.when(f_ok)
        def _():
            for t in range(2):
                kv_wait(2, t, j)
                f_copy(t, j).start()

        @pl.when(j + 1 < CHUNKS)
        def _():
            relay(j + 1)

        for side in range(2):
            @pl.when(side_ok[side])
            def _():
                q_wait(side, j)

        for slot, awaited in ((1, c >= 1), (3, (c >= 3) & jnp.logical_not(relay_ok))):
            @pl.when(awaited)
            def _():
                for t in range(2):
                    kv_wait(slot, t, j)

        lane = lax.broadcasted_iota(jnp.int32, (3 * TILE, TILE), 1)
        marks = jnp.zeros((3 * TILE, TILE), jnp.float32)
        for h in range(heads):
            at = pl.ds(pl.multiple_of(j * span + h * HEAD, HEAD), HEAD)
            q = qbuf[:, at]
            scores = []
            top = None
            for d in range(SLOTS):
                part = lax.dot_general(
                    q, kv[0, d * TILE:(d + 1) * TILE, at], (((1,), (1,)), ((), ())),
                    preferred_element_type=jnp.float32,
                )
                top = part if d == 0 else jnp.maximum(top, part + bias[d])
                scores.append(part)
            peak = jnp.max(top, axis=1, keepdims=True) * RATE
            total = None
            weights = []
            for d in range(SLOTS):
                shift = -peak if d == 0 else bias[d] - peak
                weight = jnp.exp2(scores[d] * RATE + shift)
                total = weight if total is None else total + weight
                weights.append(weight.astype(jnp.bfloat16))
            total = jnp.sum(total, axis=1, keepdims=True)
            numer = jnp.dot(
                jnp.concatenate(weights, axis=1), kv[1, :, at], preferred_element_type=jnp.float32
            )
            own_o[:, at] = numer[TILE:2 * TILE]
            send_o[0, :, at] = numer[:TILE].astype(jnp.bfloat16)
            send_o[1, :, at] = numer[2 * TILE:].astype(jnp.bfloat16)
            marks = jnp.where(lane == h, peak, marks)
            marks = jnp.where(lane == heads + h, total, marks)
        stats = marks.T[:8]
        own_st[j] = stats[:, TILE:2 * TILE]
        send_st[0, j] = stats[:, :TILE]
        send_st[1, j] = stats[:, 2 * TILE:]
        for side in range(2):
            @pl.when(side_ok[side])
            def _():
                for copy in o_copies(side, j):
                    copy.start()
        return carry

    lax.fori_loop(0, CHUNKS, attend, 0)

    locals_[3].wait()
    allowed = (
        side_ok[0] & (mask_ref[0] == 1),
        side_ok[1] & (mask_ref[2] == 1),
    )
    noise = noise_ref[0]
    gate = gate_ref[0:1, :]
    for level in range(1, gate_ref.shape[0]):
        gate = jnp.where(noise == level, gate_ref[level:level + 1, :], gate)

    projected = jnp.zeros((TILE, wbuf.shape[1]), jnp.float32)
    for j in range(CHUNKS):
        for side in range(2):
            @pl.when(side_ok[side])
            def _():
                o_wait(side, j)
        shares = []
        for h in range(heads):
            mine = own_st[j, h:h + 1, :]
            tops = [
                jnp.where(allowed[side], got_st[side, j, h:h + 1, :], LOW) for side in range(2)
            ]
            peak = jnp.maximum(mine, jnp.maximum(tops[0], tops[1]))
            factors = [jnp.exp2(top - peak) for top in (mine, *tops)]
            total = factors[0] * own_st[j, heads + h:heads + h + 1, :]
            for side in range(2):
                total = total + factors[1 + side] * got_st[side, j, heads + h:heads + h + 1, :]
            shares += [factor / total for factor in factors]
        filler = [jnp.zeros((TILE - 3 * heads, TILE), jnp.float32)]
        shares = jnp.concatenate(shares + filler, axis=0).T
        merged = []
        for h in range(heads):
            at = slice(j * span + h * HEAD, j * span + (h + 1) * HEAD)
            numer = shares[:, 3 * h:3 * h + 1] * own_o[:, at]
            for side in range(2):
                share = shares[:, 3 * h + 1 + side:3 * h + 2 + side]
                numer = numer + share * got_o[side, :, at].astype(jnp.float32)
            merged.append(numer.astype(jnp.bfloat16))
        projected = projected + jnp.dot(
            jnp.concatenate(merged, axis=1), wbuf[j * span:(j + 1) * span, :],
            preferred_element_type=jnp.float32,
        )
    out_ref[...] = (gate * projected).astype(out_ref.dtype)

    for j in range(CHUNKS - AHEAD, CHUNKS):
        wait_sends(j)

    def drain(j, carry):
        @pl.when(relay_ok)
        def _():
            for t in range(2):
                r_copy(t, j).wait_send()

        @pl.when(b_ok)
        def _():
            for t in range(2):
                b_copy(t, j).wait_send()

        @pl.when(f_ok)
        def _():
            for t in range(2):
                f_copy(t, j).wait_send()

        for side in range(2):
            @pl.when(side_ok[side])
            def _():
                for copy in o_copies(side, j):
                    copy.wait_send()
        return carry

    lax.fori_loop(0, CHUNKS, drain, 0)


def on_device(
    groups, spaces,
    query, key_new, value_new, key_clean, value_clean, out_weight, step_gate, noise_step, tile_mask,
):
    width = query.shape[2]
    anywhere = pl.BlockSpec(memory_space=pl.ANY)
    vmem = pl.BlockSpec(memory_space=pltpu.VMEM)
    smem = pl.BlockSpec(memory_space=pltpu.SMEM)
    dma = pltpu.SemaphoreType.DMA
    out = pl.pallas_call(
        functools.partial(kernel, groups, spaces),
        out_shape=pltpu.VMEM((TILE, out_weight.shape[1]), jnp.bfloat16),
        in_specs=[anywhere] * 6 + [vmem, smem, smem],
        out_specs=vmem,
        scratch_shapes=[
            pltpu.VMEM((3 * TILE, width), jnp.bfloat16),
            pltpu.VMEM((2, SLOTS * TILE, width), jnp.bfloat16),
            pltpu.VMEM(out_weight.shape, jnp.bfloat16),
            pltpu.VMEM((TILE, width), jnp.float32),
            pltpu.VMEM((CHUNKS, 8, TILE), jnp.float32),
            pltpu.VMEM((2, TILE, width), jnp.bfloat16),
            pltpu.VMEM((2, CHUNKS, 8, TILE), jnp.float32),
            pltpu.VMEM((2, TILE, width), jnp.bfloat16),
            pltpu.VMEM((2, CHUNKS, 8, TILE), jnp.float32),
            dma((4,)),
            dma((2, CHUNKS)), dma((2, CHUNKS)),
            dma((PAST, 2, CHUNKS)),
            dma((2, CHUNKS)), dma((2, CHUNKS)), dma((2, CHUNKS)), dma((2, CHUNKS)),
            dma((2, CHUNKS)), dma((2, CHUNKS)),
            dma((2, CHUNKS)), dma((2, CHUNKS)),
        ],
        compiler_params=pltpu.CompilerParams(
            collective_id=0, has_side_effects=True, vmem_limit_bytes=56 * 2**20
        ),
        name="tile_attention",
    )(
        query[0], key_new[0], value_new[0], key_clean[0], value_clean[0], out_weight,
        step_gate, noise_step, tile_mask.reshape(-1),
    )
    return out[None]


def solution(mesh):
    split = P("tm", "space", None)
    placed = (split, split, split, split, split, P(), P(), P("tm"), split)
    return jax.shard_map(
        functools.partial(on_device, mesh.shape["tm"], mesh.shape["space"]),
        mesh=mesh, in_specs=placed, out_specs=split, check_vma=False,
    )
```

```python
import functools
import math

import jax
import jax.numpy as jnp
from jax import lax
from jax.experimental import pallas as pl
from jax.experimental.pallas import tpu as pltpu
from jax.sharding import PartitionSpec as P

HEAD = 128
TILE = 128
PAST = 3
SLOTS = PAST + 1
CHUNKS = 4
AHEAD = 2
LOW = -1e30
RATE = math.log2(math.e) / math.sqrt(HEAD)
MESH = pl.DeviceIdType.MESH


def kernel(
    groups, spaces,
    q_hbm, kn_hbm, vn_hbm, kc_hbm, vc_hbm, w_hbm, gate_ref, noise_ref, mask_ref,
    out_ref,
    qbuf, kv, wbuf, own_o, own_st, send_o, send_st, got_o, got_st,
    local_sem, q_send, q_recv, kv_recv, a_send, b_send, f_send, r_send, o_send, o_recv, st_send, st_recv,
):
    c = lax.axis_index("tm")
    s = lax.axis_index("space")
    parity = lax.rem(c, 2)
    width = q_hbm.shape[1]
    span = width // CHUNKS
    heads = span // HEAD
    cleans = (kc_hbm, vc_hbm)

    locals_ = [
        pltpu.make_async_copy(q_hbm, qbuf.at[pl.ds(TILE, TILE)], local_sem.at[0]),
        pltpu.make_async_copy(kn_hbm, kv.at[0, pl.ds(0, TILE)], local_sem.at[1]),
        pltpu.make_async_copy(vn_hbm, kv.at[1, pl.ds(0, TILE)], local_sem.at[2]),
        pltpu.make_async_copy(w_hbm, wbuf, local_sem.at[3]),
    ]
    for copy in locals_:
        copy.start()

    sibling = c + 1 - 2 * parity
    far = c - 3 + 6 * parity
    corner = lax.rem(c, 4)
    a_ok = (c + 2 < groups) & jnp.logical_not((corner == 3) & (c + 3 < groups))
    relay_ok = (corner == 2) & (c >= 3)
    relayed = (corner == 1) & (c >= 2) & (c + 1 < groups)
    partners = [
        (None, {"tm": sibling}),
        ((c >= 2) & jnp.logical_not(relayed), {"tm": c - 2}),
        (a_ok, {"tm": c + 2}),
        (relay_ok, {"tm": c - 1}),
        (relayed, {"tm": c + 1}),
        ((far >= 0) & (far < groups), {"tm": far}),
        (s >= 1, {"space": s - 1}),
        (s + 1 < spaces, {"space": s + 1}),
    ]
    barrier = pltpu.get_barrier_semaphore()
    for valid, where in partners:
        def greet(where=where):
            pl.semaphore_signal(barrier, inc=1, device_id=where, device_id_type=MESH)
        if valid is None:
            greet()
        else:
            pl.when(valid)(greet)
    count = 1
    for valid, _ in partners[1:]:
        count = count + valid.astype(jnp.int32)
    pl.semaphore_wait(barrier, count)

    def columns(j):
        return pl.ds(pl.multiple_of(j * span, span), span)

    def remote(src, dst, send, recv, where):
        return pltpu.make_async_remote_copy(
            src_ref=src, dst_ref=dst, send_sem=send, recv_sem=recv,
            device_id=where, device_id_type=MESH,
        )

    def slot_rows(slot):
        return pl.ds(pl.multiple_of(slot * TILE, TILE), TILE)

    side_ok = (s >= 1, s + 1 < spaces)
    side_id = ({"space": s - 1}, {"space": s + 1})

    def q_copy(side, j):
        other = 1 - side
        return remote(
            q_hbm.at[:, columns(j)],
            qbuf.at[pl.ds(other * 2 * TILE, TILE), columns(j)],
            q_send.at[side, j], q_recv.at[other, j], side_id[side],
        )

    def q_wait(side, j):
        remote(
            q_hbm.at[:, columns(j)],
            qbuf.at[pl.ds(side * 2 * TILE, TILE), columns(j)],
            q_send.at[side, j], q_recv.at[side, j], side_id[side],
        ).wait_recv()

    to_b = c + 1 + 2 * parity
    slot_b = 1 + 2 * parity
    slot_f = 3 - 2 * parity
    b_ok = to_b < groups
    f_ok = c >= 2

    def a_copy(t, j):
        return remote(
            cleans[t].at[:, columns(j)], kv.at[t, pl.ds(2 * TILE, TILE), columns(j)],
            a_send.at[t, j], kv_recv.at[1, t, j], {"tm": c + 2},
        )

    def b_copy(t, j):
        return remote(
            cleans[t].at[:, columns(j)], kv.at[t, slot_rows(slot_b), columns(j)],
            b_send.at[t, j], kv_recv.at[slot_b - 1, t, j], {"tm": to_b},
        )

    def f_copy(t, j):
        return remote(
            kv.at[t, pl.ds(2 * TILE, TILE), columns(j)], kv.at[t, slot_rows(slot_f), columns(j)],
            f_send.at[t, j], kv_recv.at[slot_f - 1, t, j], {"tm": sibling},
        )

    def r_copy(t, j):
        return remote(
            kv.at[t, pl.ds(3 * TILE, TILE), columns(j)], kv.at[t, pl.ds(2 * TILE, TILE), columns(j)],
            r_send.at[t, j], kv_recv.at[1, t, j], {"tm": c - 1},
        )

    def kv_wait(slot, t, j):
        remote(
            cleans[t].at[:, columns(j)], kv.at[t, pl.ds(slot * TILE, TILE), columns(j)],
            a_send.at[t, j], kv_recv.at[slot - 1, t, j], {"tm": sibling},
        ).wait_recv()

    def o_rows(j):
        return pl.ds(pl.multiple_of(j * span, span), span)

    def o_copies(side, j):
        other = 1 - side
        return (
            remote(
                send_o.at[side, o_rows(j)], got_o.at[other, o_rows(j)],
                o_send.at[side, j], o_recv.at[other, j], side_id[side],
            ),
            remote(
                send_st.at[side, j], got_st.at[other, j],
                st_send.at[side, j], st_recv.at[other, j], side_id[side],
            ),
        )

    def o_wait(side, j):
        remote(
            send_o.at[side, o_rows(j)], got_o.at[side, o_rows(j)],
            o_send.at[side, j], o_recv.at[side, j], side_id[side],
        ).wait_recv()
        remote(
            send_st.at[side, j], got_st.at[side, j],
            st_send.at[side, j], st_recv.at[side, j], side_id[side],
        ).wait_recv()

    def start_sends(j):
        @pl.when(a_ok)
        def _():
            for t in range(2):
                a_copy(t, j).start()

        for side in range(2):
            @pl.when(side_ok[side])
            def _():
                q_copy(side, j).start()

    def wait_sends(j):
        @pl.when(a_ok)
        def _():
            for t in range(2):
                a_copy(t, j).wait_send()

        for side in range(2):
            @pl.when(side_ok[side])
            def _():
                q_copy(side, j).wait_send()

    for j in range(CHUNKS):
        @pl.when(b_ok)
        def _():
            for t in range(2):
                b_copy(t, j).start()

        if j < AHEAD:
            start_sends(j)

    for slot in range(1, SLOTS):
        @pl.when(c < slot)
        def _():
            kv[:, slot * TILE:(slot + 1) * TILE, :] = jnp.zeros((2, TILE, width), kv.dtype)
    for side in range(2):
        @pl.when(jnp.logical_not(side_ok[side]))
        def _():
            qbuf[side * 2 * TILE:side * 2 * TILE + TILE, :] = jnp.zeros((TILE, width), qbuf.dtype)
            got_o[side] = jnp.zeros(got_o.shape[1:], got_o.dtype)
            got_st[side] = jnp.zeros(got_st.shape[1:], got_st.dtype)

    for copy in locals_[:3]:
        copy.wait()

    bias = [None] + [jnp.where(c >= d, 0.0, LOW).astype(jnp.float32) for d in range(1, SLOTS)]

    def relay(j):
        @pl.when(relay_ok)
        def _():
            for t in range(2):
                kv_wait(3, t, j)
                r_copy(t, j).start()

    relay(0)

    def attend(j, carry):
        @pl.when(j + AHEAD < CHUNKS)
        def _():
            wait_sends(j)
            start_sends(j + AHEAD)

        @pl.when(f_ok)
        def _():
            for t in range(2):
                kv_wait(2, t, j)
                f_copy(t, j).start()

        @pl.when(j + 1 < CHUNKS)
        def _():
            relay(j + 1)

        for side in range(2):
            @pl.when(side_ok[side])
            def _():
                q_wait(side, j)

        for slot, awaited in ((1, c >= 1), (3, (c >= 3) & jnp.logical_not(relay_ok))):
            @pl.when(awaited)
            def _():
                for t in range(2):
                    kv_wait(slot, t, j)

        peaks, sums = [], []
        for h in range(heads):
            at = pl.multiple_of(j * span + h * HEAD, HEAD)
            q = qbuf[:, pl.ds(at, HEAD)]
            scores = []
            peak = None
            for d in range(SLOTS):
                k = kv[0, d * TILE:(d + 1) * TILE, pl.ds(at, HEAD)]
                part = lax.dot_general(
                    k, q, (((1,), (1,)), ((), ())), preferred_element_type=jnp.float32
                )
                top = jnp.max(part, axis=0, keepdims=True) * RATE
                if d > 0:
                    top = top + bias[d]
                peak = top if peak is None else jnp.maximum(peak, top)
                scores.append(part)
            total = None
            weights = []
            for d in range(SLOTS):
                shift = -peak if d == 0 else bias[d] - peak
                weight = jnp.exp2(scores[d] * RATE + shift)
                part = jnp.sum(weight, axis=0, keepdims=True)
                total = part if total is None else total + part
                weights.append(weight.astype(jnp.bfloat16))
            v = kv[1, :, pl.ds(at, HEAD)]
            numer = jnp.dot(
                v.T, jnp.concatenate(weights, axis=0), preferred_element_type=jnp.float32
            )
            rows = pl.ds(at, HEAD)
            own_o[rows, :] = numer[:, TILE:2 * TILE]
            send_o[0, rows, :] = numer[:, :TILE].astype(jnp.bfloat16)
            send_o[1, rows, :] = numer[:, 2 * TILE:].astype(jnp.bfloat16)
            peaks.append(peak)
            sums.append(total)
        filler = [jnp.zeros((8 - 2 * heads, 3 * TILE), jnp.float32)]
        stats = jnp.concatenate(peaks + sums + filler, axis=0)
        own_st[j] = stats[:, TILE:2 * TILE]
        send_st[0, j] = stats[:, :TILE]
        send_st[1, j] = stats[:, 2 * TILE:]
        for side in range(2):
            @pl.when(side_ok[side])
            def _():
                for copy in o_copies(side, j):
                    copy.start()
        return carry

    lax.fori_loop(0, CHUNKS, attend, 0)

    locals_[3].wait()
    allowed = (
        side_ok[0] & (mask_ref[0] == 1),
        side_ok[1] & (mask_ref[2] == 1),
    )
    noise = noise_ref[0]
    gate = gate_ref[0:1, :]
    for level in range(1, gate_ref.shape[0]):
        gate = jnp.where(noise == level, gate_ref[level:level + 1, :], gate)

    projected = jnp.zeros((TILE, wbuf.shape[1]), jnp.float32)
    for j in range(CHUNKS):
        for side in range(2):
            @pl.when(side_ok[side])
            def _():
                o_wait(side, j)
        merged = []
        for h in range(heads):
            rows = slice(j * span + h * HEAD, j * span + (h + 1) * HEAD)
            mine = own_st[j, h:h + 1, :]
            tops = [
                jnp.where(allowed[side], got_st[side, j, h:h + 1, :], LOW) for side in range(2)
            ]
            peak = jnp.maximum(mine, jnp.maximum(tops[0], tops[1]))
            factor = jnp.exp2(mine - peak)
            total = factor * own_st[j, heads + h:heads + h + 1, :]
            numer = factor * own_o[rows, :]
            for side in range(2):
                factor = jnp.exp2(tops[side] - peak)
                total = total + factor * got_st[side, j, heads + h:heads + h + 1, :]
                numer = numer + factor * got_o[side, rows, :].astype(jnp.float32)
            merged.append((numer / total).T.astype(jnp.bfloat16))
        projected = projected + jnp.dot(
            jnp.concatenate(merged, axis=1), wbuf[j * span:(j + 1) * span, :],
            preferred_element_type=jnp.float32,
        )
    out_ref[...] = (gate * projected).astype(out_ref.dtype)

    for j in range(CHUNKS - AHEAD, CHUNKS):
        wait_sends(j)

    def drain(j, carry):
        @pl.when(relay_ok)
        def _():
            for t in range(2):
                r_copy(t, j).wait_send()

        @pl.when(b_ok)
        def _():
            for t in range(2):
                b_copy(t, j).wait_send()

        @pl.when(f_ok)
        def _():
            for t in range(2):
                f_copy(t, j).wait_send()

        for side in range(2):
            @pl.when(side_ok[side])
            def _():
                for copy in o_copies(side, j):
                    copy.wait_send()
        return carry

    lax.fori_loop(0, CHUNKS, drain, 0)


def on_device(
    groups, spaces,
    query, key_new, value_new, key_clean, value_clean, out_weight, step_gate, noise_step, tile_mask,
):
    width = query.shape[2]
    anywhere = pl.BlockSpec(memory_space=pl.ANY)
    vmem = pl.BlockSpec(memory_space=pltpu.VMEM)
    smem = pl.BlockSpec(memory_space=pltpu.SMEM)
    dma = pltpu.SemaphoreType.DMA
    out = pl.pallas_call(
        functools.partial(kernel, groups, spaces),
        out_shape=pltpu.VMEM((TILE, out_weight.shape[1]), jnp.bfloat16),
        in_specs=[anywhere] * 6 + [vmem, smem, smem],
        out_specs=vmem,
        scratch_shapes=[
            pltpu.VMEM((3 * TILE, width), jnp.bfloat16),
            pltpu.VMEM((2, SLOTS * TILE, width), jnp.bfloat16),
            pltpu.VMEM(out_weight.shape, jnp.bfloat16),
            pltpu.VMEM((width, TILE), jnp.float32),
            pltpu.VMEM((CHUNKS, 8, TILE), jnp.float32),
            pltpu.VMEM((2, width, TILE), jnp.bfloat16),
            pltpu.VMEM((2, CHUNKS, 8, TILE), jnp.float32),
            pltpu.VMEM((2, width, TILE), jnp.bfloat16),
            pltpu.VMEM((2, CHUNKS, 8, TILE), jnp.float32),
            dma((4,)),
            dma((2, CHUNKS)), dma((2, CHUNKS)),
            dma((PAST, 2, CHUNKS)),
            dma((2, CHUNKS)), dma((2, CHUNKS)), dma((2, CHUNKS)), dma((2, CHUNKS)),
            dma((2, CHUNKS)), dma((2, CHUNKS)),
            dma((2, CHUNKS)), dma((2, CHUNKS)),
        ],
        compiler_params=pltpu.CompilerParams(
            collective_id=0, has_side_effects=True, vmem_limit_bytes=56 * 2**20
        ),
        name="tile_attention",
    )(
        query[0], key_new[0], value_new[0], key_clean[0], value_clean[0], out_weight,
        step_gate, noise_step, tile_mask.reshape(-1),
    )
    return out[None]


def solution(mesh):
    split = P("tm", "space", None)
    placed = (split, split, split, split, split, P(), P(), P("tm"), split)
    return jax.shard_map(
        functools.partial(on_device, mesh.shape["tm"], mesh.shape["space"]),
        mesh=mesh, in_specs=placed, out_specs=split, check_vma=False,
    )
```

```python
import functools
import math

import jax
import jax.numpy as jnp
from jax import lax
from jax.experimental import pallas as pl
from jax.experimental.pallas import tpu as pltpu
from jax.sharding import PartitionSpec as P

HEAD = 128
TILE = 128
PAST = 3
SLOTS = PAST + 1
CHUNKS = 4
AHEAD = 2
LOW = -1e30
RATE = math.log2(math.e) / math.sqrt(HEAD)
MESH = pl.DeviceIdType.MESH


def kernel(
    groups, spaces,
    q_hbm, kn_hbm, vn_hbm, kc_hbm, vc_hbm, w_hbm, gate_ref, noise_ref, mask_ref,
    out_ref,
    qbuf, kv, wbuf, own_o, own_st, send_o, send_st, got_o, got_st,
    local_sem, q_send, q_recv, kv_recv, a_send, b_send, f_send, r_send, o_send, o_recv, st_send, st_recv,
):
    c = lax.axis_index("tm")
    s = lax.axis_index("space")
    parity = lax.rem(c, 2)
    width = q_hbm.shape[1]
    span = width // CHUNKS
    heads = span // HEAD
    cleans = (kc_hbm, vc_hbm)

    sibling = c + 1 - 2 * parity
    far = c - 3 + 6 * parity
    corner = lax.rem(c, 4)
    a_ok = (c + 2 < groups) & jnp.logical_not((corner == 3) & (c + 3 < groups))
    relay_ok = (corner == 2) & (c >= 3)
    relayed = (corner == 1) & (c >= 2) & (c + 1 < groups)
    partners = [
        (None, {"tm": sibling}),
        ((c >= 2) & jnp.logical_not(relayed), {"tm": c - 2}),
        (a_ok, {"tm": c + 2}),
        (relay_ok, {"tm": c - 1}),
        (relayed, {"tm": c + 1}),
        ((far >= 0) & (far < groups), {"tm": far}),
        (s >= 1, {"space": s - 1}),
        (s + 1 < spaces, {"space": s + 1}),
    ]
    barrier = pltpu.get_barrier_semaphore()
    for valid, where in partners:
        def greet(where=where):
            pl.semaphore_signal(barrier, inc=1, device_id=where, device_id_type=MESH)
        if valid is None:
            greet()
        else:
            pl.when(valid)(greet)
    locals_ = [
        pltpu.make_async_copy(q_hbm, qbuf.at[pl.ds(TILE, TILE)], local_sem.at[0]),
        pltpu.make_async_copy(kn_hbm, kv.at[0, pl.ds(0, TILE)], local_sem.at[1]),
        pltpu.make_async_copy(vn_hbm, kv.at[1, pl.ds(0, TILE)], local_sem.at[2]),
        pltpu.make_async_copy(w_hbm, wbuf, local_sem.at[3]),
    ]
    for copy in locals_:
        copy.start()

    count = 1
    for valid, _ in partners[1:]:
        count = count + valid.astype(jnp.int32)
    pl.semaphore_wait(barrier, count)

    def columns(j):
        return pl.ds(pl.multiple_of(j * span, span), span)

    def remote(src, dst, send, recv, where):
        return pltpu.make_async_remote_copy(
            src_ref=src, dst_ref=dst, send_sem=send, recv_sem=recv,
            device_id=where, device_id_type=MESH,
        )

    def slot_rows(slot):
        return pl.ds(pl.multiple_of(slot * TILE, TILE), TILE)

    side_ok = (s >= 1, s + 1 < spaces)
    side_id = ({"space": s - 1}, {"space": s + 1})

    def q_copy(side, j):
        other = 1 - side
        return remote(
            q_hbm.at[:, columns(j)],
            qbuf.at[pl.ds(other * 2 * TILE, TILE), columns(j)],
            q_send.at[side, j], q_recv.at[other, j], side_id[side],
        )

    def q_wait(side, j):
        remote(
            q_hbm.at[:, columns(j)],
            qbuf.at[pl.ds(side * 2 * TILE, TILE), columns(j)],
            q_send.at[side, j], q_recv.at[side, j], side_id[side],
        ).wait_recv()

    to_b = c + 1 + 2 * parity
    slot_b = 1 + 2 * parity
    slot_f = 3 - 2 * parity
    b_ok = to_b < groups
    f_ok = c >= 2

    def a_copy(t, j):
        return remote(
            cleans[t].at[:, columns(j)], kv.at[t, pl.ds(2 * TILE, TILE), columns(j)],
            a_send.at[t, j], kv_recv.at[1, t, j], {"tm": c + 2},
        )

    def b_copy(t, j):
        return remote(
            cleans[t].at[:, columns(j)], kv.at[t, slot_rows(slot_b), columns(j)],
            b_send.at[t, j], kv_recv.at[slot_b - 1, t, j], {"tm": to_b},
        )

    def f_copy(t, j):
        return remote(
            kv.at[t, pl.ds(2 * TILE, TILE), columns(j)], kv.at[t, slot_rows(slot_f), columns(j)],
            f_send.at[t, j], kv_recv.at[slot_f - 1, t, j], {"tm": sibling},
        )

    def r_copy(t, j):
        return remote(
            kv.at[t, pl.ds(3 * TILE, TILE), columns(j)], kv.at[t, pl.ds(2 * TILE, TILE), columns(j)],
            r_send.at[t, j], kv_recv.at[1, t, j], {"tm": c - 1},
        )

    def kv_wait(slot, t, j):
        remote(
            cleans[t].at[:, columns(j)], kv.at[t, pl.ds(slot * TILE, TILE), columns(j)],
            a_send.at[t, j], kv_recv.at[slot - 1, t, j], {"tm": sibling},
        ).wait_recv()

    def o_rows(j):
        return pl.ds(pl.multiple_of(j * span, span), span)

    def o_copies(side, j):
        other = 1 - side
        return (
            remote(
                send_o.at[side, o_rows(j)], got_o.at[other, o_rows(j)],
                o_send.at[side, j], o_recv.at[other, j], side_id[side],
            ),
            remote(
                send_st.at[side, j], got_st.at[other, j],
                st_send.at[side, j], st_recv.at[other, j], side_id[side],
            ),
        )

    def o_wait(side, j):
        remote(
            send_o.at[side, o_rows(j)], got_o.at[side, o_rows(j)],
            o_send.at[side, j], o_recv.at[side, j], side_id[side],
        ).wait_recv()
        remote(
            send_st.at[side, j], got_st.at[side, j],
            st_send.at[side, j], st_recv.at[side, j], side_id[side],
        ).wait_recv()

    def start_sends(j):
        @pl.when(a_ok)
        def _():
            for t in range(2):
                a_copy(t, j).start()

        for side in range(2):
            @pl.when(side_ok[side])
            def _():
                q_copy(side, j).start()

    def wait_sends(j):
        @pl.when(a_ok)
        def _():
            for t in range(2):
                a_copy(t, j).wait_send()

        for side in range(2):
            @pl.when(side_ok[side])
            def _():
                q_copy(side, j).wait_send()

    for j in range(CHUNKS):
        if j < AHEAD:
            start_sends(j)

        @pl.when(b_ok)
        def _():
            for t in range(2):
                b_copy(t, j).start()

    for slot in range(1, SLOTS):
        @pl.when(c < slot)
        def _():
            kv[:, slot * TILE:(slot + 1) * TILE, :] = jnp.zeros((2, TILE, width), kv.dtype)
    for side in range(2):
        @pl.when(jnp.logical_not(side_ok[side]))
        def _():
            qbuf[side * 2 * TILE:side * 2 * TILE + TILE, :] = jnp.zeros((TILE, width), qbuf.dtype)
            got_o[side] = jnp.zeros(got_o.shape[1:], got_o.dtype)
            got_st[side] = jnp.zeros(got_st.shape[1:], got_st.dtype)

    for copy in locals_[:3]:
        copy.wait()

    bias = [None] + [jnp.where(c >= d, 0.0, LOW).astype(jnp.float32) for d in range(1, SLOTS)]

    def relay(j):
        @pl.when(relay_ok)
        def _():
            for t in range(2):
                kv_wait(3, t, j)
                r_copy(t, j).start()

    relay(0)

    def attend(j, carry):
        @pl.when(j + AHEAD < CHUNKS)
        def _():
            wait_sends(j)
            start_sends(j + AHEAD)

        @pl.when(f_ok)
        def _():
            for t in range(2):
                kv_wait(2, t, j)
                f_copy(t, j).start()

        @pl.when(j + 1 < CHUNKS)
        def _():
            relay(j + 1)

        for side in range(2):
            @pl.when(side_ok[side])
            def _():
                q_wait(side, j)

        for slot, awaited in ((1, c >= 1), (3, (c >= 3) & jnp.logical_not(relay_ok))):
            @pl.when(awaited)
            def _():
                for t in range(2):
                    kv_wait(slot, t, j)

        peaks, sums = [], []
        for h in range(heads):
            at = pl.multiple_of(j * span + h * HEAD, HEAD)
            q = qbuf[:, pl.ds(at, HEAD)]
            scores = []
            peak = None
            for d in range(SLOTS):
                k = kv[0, d * TILE:(d + 1) * TILE, pl.ds(at, HEAD)]
                part = lax.dot_general(
                    k, q, (((1,), (1,)), ((), ())), preferred_element_type=jnp.float32
                )
                top = jnp.max(part, axis=0, keepdims=True) * RATE
                if d > 0:
                    top = top + bias[d]
                peak = top if peak is None else jnp.maximum(peak, top)
                scores.append(part)
            total = None
            weights = []
            for d in range(SLOTS):
                shift = -peak if d == 0 else bias[d] - peak
                weight = jnp.exp2(scores[d] * RATE + shift)
                part = jnp.sum(weight, axis=0, keepdims=True)
                total = part if total is None else total + part
                weights.append(weight.astype(jnp.bfloat16))
            v = kv[1, :, pl.ds(at, HEAD)]
            numer = jnp.dot(
                v.T, jnp.concatenate(weights, axis=0), preferred_element_type=jnp.float32
            )
            rows = pl.ds(at, HEAD)
            own_o[rows, :] = numer[:, TILE:2 * TILE]
            send_o[0, rows, :] = numer[:, :TILE].astype(jnp.bfloat16)
            send_o[1, rows, :] = numer[:, 2 * TILE:].astype(jnp.bfloat16)
            peaks.append(peak)
            sums.append(total)
        filler = [jnp.zeros((8 - 2 * heads, 3 * TILE), jnp.float32)]
        stats = jnp.concatenate(peaks + sums + filler, axis=0)
        own_st[j] = stats[:, TILE:2 * TILE]
        send_st[0, j] = stats[:, :TILE]
        send_st[1, j] = stats[:, 2 * TILE:]
        for side in range(2):
            @pl.when(side_ok[side])
            def _():
                for copy in o_copies(side, j):
                    copy.start()
        return carry

    lax.fori_loop(0, CHUNKS, attend, 0)

    locals_[3].wait()
    allowed = (
        side_ok[0] & (mask_ref[0] == 1),
        side_ok[1] & (mask_ref[2] == 1),
    )
    noise = noise_ref[0]
    gate = gate_ref[0:1, :]
    for level in range(1, gate_ref.shape[0]):
        gate = jnp.where(noise == level, gate_ref[level:level + 1, :], gate)

    projected = jnp.zeros((TILE, wbuf.shape[1]), jnp.float32)
    for j in range(CHUNKS):
        for side in range(2):
            @pl.when(side_ok[side])
            def _():
                o_wait(side, j)
        merged = []
        for h in range(heads):
            rows = slice(j * span + h * HEAD, j * span + (h + 1) * HEAD)
            mine = own_st[j, h:h + 1, :]
            tops = [
                jnp.where(allowed[side], got_st[side, j, h:h + 1, :], LOW) for side in range(2)
            ]
            peak = jnp.maximum(mine, jnp.maximum(tops[0], tops[1]))
            factor = jnp.exp2(mine - peak)
            total = factor * own_st[j, heads + h:heads + h + 1, :]
            numer = factor * own_o[rows, :]
            for side in range(2):
                factor = jnp.exp2(tops[side] - peak)
                total = total + factor * got_st[side, j, heads + h:heads + h + 1, :]
                numer = numer + factor * got_o[side, rows, :].astype(jnp.float32)
            merged.append((numer / total).T.astype(jnp.bfloat16))
        projected = projected + jnp.dot(
            jnp.concatenate(merged, axis=1), wbuf[j * span:(j + 1) * span, :],
            preferred_element_type=jnp.float32,
        )
    out_ref[...] = (gate * projected).astype(out_ref.dtype)

    for j in range(CHUNKS - AHEAD, CHUNKS):
        wait_sends(j)

    def drain(j, carry):
        @pl.when(relay_ok)
        def _():
            for t in range(2):
                r_copy(t, j).wait_send()

        @pl.when(b_ok)
        def _():
            for t in range(2):
                b_copy(t, j).wait_send()

        @pl.when(f_ok)
        def _():
            for t in range(2):
                f_copy(t, j).wait_send()

        for side in range(2):
            @pl.when(side_ok[side])
            def _():
                for copy in o_copies(side, j):
                    copy.wait_send()
        return carry

    lax.fori_loop(0, CHUNKS, drain, 0)


def on_device(
    groups, spaces,
    query, key_new, value_new, key_clean, value_clean, out_weight, step_gate, noise_step, tile_mask,
):
    width = query.shape[2]
    anywhere = pl.BlockSpec(memory_space=pl.ANY)
    vmem = pl.BlockSpec(memory_space=pltpu.VMEM)
    smem = pl.BlockSpec(memory_space=pltpu.SMEM)
    dma = pltpu.SemaphoreType.DMA
    out = pl.pallas_call(
        functools.partial(kernel, groups, spaces),
        out_shape=pltpu.VMEM((TILE, out_weight.shape[1]), jnp.bfloat16),
        in_specs=[anywhere] * 6 + [vmem, smem, smem],
        out_specs=vmem,
        scratch_shapes=[
            pltpu.VMEM((3 * TILE, width), jnp.bfloat16),
            pltpu.VMEM((2, SLOTS * TILE, width), jnp.bfloat16),
            pltpu.VMEM(out_weight.shape, jnp.bfloat16),
            pltpu.VMEM((width, TILE), jnp.float32),
            pltpu.VMEM((CHUNKS, 8, TILE), jnp.float32),
            pltpu.VMEM((2, width, TILE), jnp.bfloat16),
            pltpu.VMEM((2, CHUNKS, 8, TILE), jnp.float32),
            pltpu.VMEM((2, width, TILE), jnp.bfloat16),
            pltpu.VMEM((2, CHUNKS, 8, TILE), jnp.float32),
            dma((4,)),
            dma((2, CHUNKS)), dma((2, CHUNKS)),
            dma((PAST, 2, CHUNKS)),
            dma((2, CHUNKS)), dma((2, CHUNKS)), dma((2, CHUNKS)), dma((2, CHUNKS)),
            dma((2, CHUNKS)), dma((2, CHUNKS)),
            dma((2, CHUNKS)), dma((2, CHUNKS)),
        ],
        compiler_params=pltpu.CompilerParams(
            collective_id=0, has_side_effects=True, vmem_limit_bytes=56 * 2**20
        ),
        name="tile_attention",
    )(
        query[0], key_new[0], value_new[0], key_clean[0], value_clean[0], out_weight,
        step_gate, noise_step, tile_mask.reshape(-1),
    )
    return out[None]


def solution(mesh):
    split = P("tm", "space", None)
    placed = (split, split, split, split, split, P(), P(), P("tm"), split)
    return jax.shard_map(
        functools.partial(on_device, mesh.shape["tm"], mesh.shape["space"]),
        mesh=mesh, in_specs=placed, out_specs=split, check_vma=False,
    )
```
